256 devices in a mesh: row: 16 (over x, y), col: 16 (over z, core).
Axes of the slice: x: 4, y: 4, z: 8, core: 2. Of those that a mesh axis runs over, the one named last changes fastest.
Arguments:
- source: float32 [8, 8192, 4096], P(None, 'col', 'row'), may hold values from -6 to 6
- pole_x: float32 [8, 4], replicated, may hold values from 0.95 to 1, as said below
- weight_x: float32 [8, 4], replicated, may hold values from 0.15 to 0.4
- pole_y: float32 [8, 4], replicated, may hold values from 0.95 to 1, as said below
- weight_y: float32 [8, 4], replicated, may hold values from 0.15 to 0.4
Outputs:
- coefficient: float32 [8, 8192, 4096], P(None, 'col', 'row')
The draws below stay inside these ranges and needn't reach their ends.
Inputs may be any that keep to these rules, and one draw needn't show every extreme that they name: `pole_x`: each pole is below one. `pole_y`: each pole is below one.
All inputs are finite; a program needn't handle non-finite values.
Results may differ from the reference program's by a relative error of at most 0.0003.
Values sent between devices are 32-bit elements; how exact they have to be, the bound alone decides.
A program may use at most 128 MiB of HBM per device.

```python
import jax
import jax.numpy as jnp
from jax import lax

LEVELS = 8
POLES = 4
NX = 4096
NY = 8192


def pole_table(key, length):
    pick_key, slow_key, middle_key, fast_key, place_key = jax.random.split(jax.random.fold_in(key, 11), 5)
    slow_share = 0.45
    fast_share = 0.25
    picked = jax.random.uniform(pick_key, (LEVELS, POLES))
    forced_place = jax.random.randint(place_key, (LEVELS, 1), 0, POLES)
    forced = forced_place == jnp.arange(POLES)[None, :]
    slow_low = max(length / 2.0, 20.0)
    slow_high = max(2.0 * length, 60.0)
    slow_time = jnp.exp(jax.random.uniform(slow_key, (LEVELS, POLES), minval=jnp.log(slow_low), maxval=jnp.log(slow_high)))
    middle_time = jnp.exp(jax.random.uniform(middle_key, (LEVELS, POLES), minval=jnp.log(100.0), maxval=jnp.log(400.0)))
    fast_time = jnp.exp(jax.random.uniform(fast_key, (LEVELS, POLES), minval=jnp.log(20.0), maxval=jnp.log(50.0)))
    times_all = jnp.where(picked < slow_share, slow_time, jnp.where(picked < slow_share + fast_share, fast_time, middle_time))
    times_all = jnp.where(forced, middle_time, times_all)
    return jnp.exp(-1.0 / times_all).astype(jnp.float32)


def draw_pole_x(key, part):
    return pole_table(jax.random.fold_in(key, 1), NX * 1.0)


def draw_pole_y(key, part):
    return pole_table(jax.random.fold_in(key, 2), NY * 1.0)


def steps_of(stream_key, extent, shards, low, top_value):
    def one(dim, parts):
        draws = jax.random.uniform(jax.random.fold_in(jax.random.fold_in(stream_key, 6), dim), (parts,), jnp.float32, low / len(shards), top_value / len(shards))
        return jnp.repeat(jnp.exp(draws), extent[dim] // parts).reshape((-1,) + (1,) * (len(extent) - dim - 1))

    gain = one(*shards[0])
    for cut in shards[1:]:
        gain = gain * one(*cut)
    return gain


def scatter_about(rng, dims, deviation, most, shards=(), dtype=jnp.bfloat16):
    gain = steps_of(rng, dims, shards, -0.22, 0.18) if shards else 1.0
    values = jax.random.normal(rng, dims, jnp.float32) * deviation * gain
    return jnp.minimum(jnp.maximum(values, -most), most).astype(dtype)


def setup_inputs(seed: int = 0) -> dict:
    seeds = jax.random.split(jax.random.key(seed), 6)
    return {
        "source": scatter_about(seeds[0], (LEVELS, NY, NX), 1.0, 6.0, ((1, 16), (2, 16)), jnp.float32),
        "pole_x": draw_pole_x(jax.random.fold_in(seeds[5], 71), 0),
        "weight_x": jnp.clip(jax.random.uniform(seeds[2], (LEVELS, POLES), jnp.float32, 0.15, 0.4), 0.15, 0.4),
        "pole_y": draw_pole_y(jax.random.fold_in(seeds[5], 71), 0),
        "weight_y": jnp.clip(jax.random.uniform(seeds[4], (LEVELS, POLES), jnp.float32, 0.15, 0.4), 0.15, 0.4),
    }


def forward_lines(lines_in, pole_values, weights):
    gain_rate = jnp.sqrt(1.0 - pole_values * pole_values)

    def advance(carry_state, column):
        carry_state = pole_values[:, None] * carry_state + gain_rate[:, None] * column[None, :]
        return (carry_state, lax.optimization_barrier(jnp.sum(weights[:, None] * carry_state, axis=0)))
    initial = jnp.zeros((pole_values.shape[0], lines_in.shape[1]), jnp.float32)
    return lax.scan(advance, initial, lines_in)[1]

def backward_lines(lines_in, pole_values, weights):
    gain_rate = 1.0 - pole_values

    def advance(carry_state, column):
        carry_state = pole_values[:, None] * carry_state + gain_rate[:, None] * column[None, :]
        return (carry_state, lax.optimization_barrier(jnp.sum(weights[:, None] * carry_state, axis=0)))
    initial = jnp.zeros((pole_values.shape[0], lines_in.shape[1]), jnp.float32)
    return lax.scan(advance, initial, lines_in, reverse=True)[1]

def level_filter(inputs):
    source_level, pole_x, weight_x, pole_y, weight_y = inputs
    along_x = forward_lines(source_level.T, pole_x, weight_x)
    smooth_x = backward_lines(along_x, pole_x, weight_x).T
    along_y = forward_lines(smooth_x, pole_y, weight_y)
    smooth_y = backward_lines(along_y, pole_y, weight_y)
    return jnp.exp(smooth_y)

def reference(source, pole_x, weight_x, pole_y, weight_y):
    return lax.map(level_filter, (source, pole_x, weight_x, pole_y, weight_y))
```

```python
import functools

import jax
import jax.numpy as jnp
from jax import lax
from jax.experimental import pallas as pl
from jax.experimental.pallas import tpu as pltpu
from jax.sharding import PartitionSpec as P

MESH = pl.DeviceIdType.MESH
LEVELS = 8
POLES = 4
BLOCK = 256
PEERS = 16
f32 = jnp.float32
bf16 = jnp.bfloat16
NN = (((1,), (0,)), ((), ()))
NT = (((1,), (1,)), ((), ()))
TN = (((0,), (0,)), ((), ()))


def mm(a, b, dims=NN):
    return lax.dot_general(a, b, dims, preferred_element_type=f32)


def halves(value):
    high = value.astype(bf16)
    return high, (value - high.astype(f32)).astype(bf16)


def iota(shape, dim):
    return lax.broadcasted_iota(jnp.int32, shape, dim)


def log_of(short):
    total = jnp.full_like(short, 1.0 / 7.0)
    for n in (6, 5, 4, 3, 2, 1):
        total = total * short + 1.0 / n
    return -short * total


def by_pole(ref, level, shape):
    place = iota(shape, 0) % POLES
    value = jnp.full(shape, ref[level, POLES - 1], f32)
    for k in range(POLES - 1):
        value = jnp.where(place == k, ref[level, k], value)
    return value


def couplings(short, decay, weight, shift):
    gain = jnp.sqrt(1.0 - decay * decay)
    forward, backward = weight * gain, weight * short
    sum_f = jnp.zeros_like(short)
    sum_b = jnp.zeros_like(short)
    for m in range(POLES):
        short_m, f_m, b_m = (short, forward, backward) if m == 0 else tuple(shift(t, m) for t in (short, forward, backward))
        share = 1.0 / (short + short_m - short * short_m)
        sum_f += b_m * share
        sum_b += f_m * share
    return forward, sum_b, forward * sum_f, backward * sum_b


def line_tables(pole_ref, weight_ref, level):
    shape = (8, 128)
    decay, weight = by_pole(pole_ref, level, shape), by_pole(weight_ref, level, shape)
    short = 1.0 - decay
    rate = log_of(short)
    _, _, c_f, c_b = couplings(short, decay, weight, lambda t, m: pltpu.roll(t, m, 0))
    forward = iota((8, BLOCK), 0) < POLES
    place = iota((8, BLOCK), 1)
    wide = lambda t: jnp.concatenate([t, t], axis=1)
    summary = jnp.exp(wide(rate) * jnp.where(forward, BLOCK - 1 - place, place).astype(f32))
    entry = jnp.exp(wide(rate) * jnp.where(forward, place + 1, BLOCK - place).astype(f32))
    entry = entry * jnp.where(forward, wide(c_f), wide(c_b))
    return rate, c_f, c_b, summary, entry


def toeplitz(rate, low, up, store):
    shape = (8, 128)
    sub, lane = iota(shape, 0), iota(shape, 1)
    apart = (sub - lane).astype(f32)
    rates = [jnp.broadcast_to(rate[k : k + 1, :], shape) for k in range(POLES)]
    step = [jnp.exp(8.0 * r) for r in rates]
    below = [jnp.broadcast_to(low[k : k + 1, :], shape) * jnp.exp(rates[k] * apart) for k in range(POLES)]
    above = [jnp.broadcast_to(up[k : k + 1, :], shape) * jnp.exp(rates[k] * (-120.0 - apart)) for k in range(POLES)]
    upper = {}
    for m in range(15, -17, -1):
        upper[m] = (above[0] + above[1]) + (above[2] + above[3])
        above = [a * s for a, s in zip(above, step)]
    tiles = {}
    for m in range(-16, 32):
        if m < 0:
            tiles[m] = upper[m]
            continue
        lower = (below[0] + below[1]) + (below[2] + below[3])
        below = [b * s for b, s in zip(below, step)]
        tiles[m] = lower if m > 15 else jnp.where(sub + 8 * m >= lane, lower, upper[m])
    for m in range(-16, 32, 2):
        high, low_part = halves(jnp.concatenate([tiles[m], tiles[m + 1]], axis=0))
        for j in range(2):
            if 0 <= m + 16 * j < 32:
                store(8 * (m + 16 * j), 128 * j, high, low_part)


def end_mix(pole_ref, weight_ref, level, shape):
    decay, weight = by_pole(pole_ref, level, shape), by_pole(weight_ref, level, shape)
    short = 1.0 - decay
    parts, total = [], jnp.zeros(shape, f32)
    for k in range(POLES):
        p_k = jnp.full(shape, pole_ref[level, k], f32)
        q_k = 1.0 - p_k
        part = weight_ref[level, k] * jnp.sqrt(1.0 - p_k * p_k) / (short + q_k - short * q_k)
        total += part
        parts.append(part * p_k)
    return [-part / total for part in parts], log_of(short)


def scan_blocks(inputs, decay, mix):
    forward = iota(decay.shape, 0) < POLES
    state = jnp.zeros_like(decay)
    before = []
    for block in inputs:
        before.append(state)
        state = decay * state + block
    end = jnp.zeros_like(decay)
    for k in range(POLES):
        end += mix[k] * jnp.broadcast_to(state[k : k + 1, :], decay.shape)
    state = end
    out = [None] * len(inputs)
    for i in range(len(inputs) - 1, -1, -1):
        out[i] = jnp.where(forward, before[i], state)
        state = decay * state + inputs[i]
    return out


def kernel_states(
    px, wx, py, wy, u_hbm, p_hbm, left_out, right_out,
    u_v, zh_v, zl_v, ty_v, txh_v, txl_v, sx_v, sxh_v, sxl_v, ex_v, ey_v, decay_y, v_v, ys_v,
    row_out, row_in, col_out, col_in, row_out2, row_in2, col_out2, col_in2,
    load_sem, save_sem, row_send, row_recv, col_send, col_recv, row_send2, row_recv2, col_send2, col_recv2,
):
    r, c = lax.axis_index("row"), lax.axis_index("col")
    load = lambda l: pltpu.make_async_copy(u_hbm.at[l], u_v.at[l], load_sem.at[l])
    save = lambda l: pltpu.make_async_copy(u_v.at[l], p_hbm.at[l], save_sem.at[l])

    @pl.loop(0, LEVELS)
    def _(l):
        load(l).start()

    barrier = pltpu.get_barrier_semaphore()

    @pl.loop(1, PEERS)
    def _(j):
        pl.semaphore_signal(barrier, inc=1, device_id=(lax.rem(r + j, PEERS), c), device_id_type=MESH)
        pl.semaphore_signal(barrier, inc=1, device_id=(r, lax.rem(c + j, PEERS)), device_id_type=MESH)

    tile = (8, 128)

    @pl.loop(0, LEVELS)
    def _(l):
        rate, c_f, c_b, summary, entry = line_tables(px, wx, l)
        s_h, s_l = halves(summary)
        sx_v[l] = jnp.concatenate([s_h.astype(f32), s_l.astype(f32)], axis=0).astype(bf16)
        sxh_v[pl.ds(8 * l, 8), :] = s_h.astype(f32)
        sxl_v[pl.ds(8 * l, 8), :] = s_l.astype(f32)
        ex_v[l] = entry

        def store_x(row, lane, high, low):
            txh_v[l, row : row + 16, lane : lane + 128] = high
            txl_v[l, row : row + 16, lane : lane + 128] = low

        toeplitz(rate, c_b, c_f, store_x)

        rate, c_f, c_b, summary, entry = line_tables(py, wy, l)
        s_h, s_l = halves(summary)
        ty_v[l, 256:272, :] = jnp.concatenate([s_h.astype(f32), s_l.astype(f32)], axis=0).astype(bf16)
        ey_v[l] = entry
        decay_y[l] = jnp.exp(rate * BLOCK)

        def store_y(row, lane, high, low):
            ty_v[l, row : row + 16, lane : lane + 128] = high
            ty_v[l, row + 272 : row + 288, lane : lane + 128] = low

        toeplitz(rate, c_f, c_b, store_y)

    forward_wide = iota((8, BLOCK), 0) < POLES

    @pl.loop(0, LEVELS)
    def _(l):
        load(l).wait()
        sums = []
        for s in range(2):
            rows = slice(BLOCK * s, BLOCK * (s + 1))
            u_h, u_l = halves(u_v[l, rows, :])
            d1 = mm(ty_v[l], u_h)
            d2 = mm(ty_v[l, 0:272, :], u_l)
            z = d1[0:256] + d1[272:528] + d2[0:256]
            v = d1[256:264] + d1[264:272] + d2[256:264]
            z_h, z_l = halves(z)
            zh_v[l, rows, :] = z_h
            zl_v[l, rows, :] = z_l
            e1 = mm(sx_v[l], z_h, NT)
            e2 = mm(sx_v[l], z_l, NT)
            row_out[2 * l + s, :, 0:256] = e1[0:8] + e1[8:16] + e2[0:8]
            v_v[s * LEVELS + l] = v
            sums.append(v)
        v_h, v_l = halves(jnp.concatenate(sums, axis=0))
        y1 = mm(jnp.concatenate([v_h, v_l], axis=0), txh_v[l])
        y2 = mm(v_h, txl_v[l])
        ys = y1[0:16] + y1[16:32] + y2
        ys_v[l] = ys
        decay = jnp.concatenate([decay_y[l], decay_y[l]], axis=1)
        both = jnp.where(forward_wide, decay * ys[0:8] + ys[8:16], ys[0:8] + decay * ys[8:16])
        col_out[2 * l] = both[:, 0:128]
        col_out[2 * l + 1] = both[:, 128:256]

    v_h, v_l = halves(v_v[...].reshape(128, BLOCK))
    sxh = jnp.concatenate([sxh_v[...], sxh_v[...]], axis=0).astype(bf16)
    sxl = jnp.concatenate([sxl_v[...], sxl_v[...]], axis=0).astype(bf16)
    corner = mm(v_h, sxh, NT) + (mm(v_l, sxh, NT) + mm(v_h, sxl, NT))
    own = iota((128, 128), 0) // 8 == iota((128, 128), 1) // 8
    corner = jnp.sum(jnp.where(own, corner, 0.0).reshape(16, 8, 128), axis=0)

    @pl.loop(0, PEERS)
    def _(q):
        row_out[q, :, 256:384] = corner

    pl.semaphore_wait(barrier, 2 * (PEERS - 1))

    def row_copy(peer, there, src, dst, send, recv):
        return pltpu.make_async_remote_copy(
            src_ref=src.at[peer], dst_ref=dst.at[there], send_sem=send.at[peer], recv_sem=recv.at[there],
            device_id=(peer, c), device_id_type=MESH,
        )

    def col_copy(peer, there, src, dst, send, recv):
        return pltpu.make_async_remote_copy(
            src_ref=src.at[peer], dst_ref=dst.at[there], send_sem=send.at[peer], recv_sem=recv.at[there],
            device_id=(r, peer), device_id_type=MESH,
        )

    row1 = (row_out, row_in, row_send, row_recv)
    col1 = (col_out, col_in, col_send, col_recv)
    row2 = (row_out2, row_in2, row_send2, row_recv2)
    col2 = (col_out2, col_in2, col_send2, col_recv2)

    @pl.loop(1, PEERS)
    def _(j):
        row_copy(lax.rem(r + j, PEERS), r, *row1).start()
        col_copy(lax.rem(c + j, PEERS), c, *col1).start()

    row_in[r] = row_out[r]
    col_in[c] = col_out[c]

    def local_field(l):
        p = mm(zh_v[l], txh_v[l]) + (mm(zl_v[l], txh_v[l]) + mm(zh_v[l], txl_v[l]))
        u_v[l] = p
        save(l).start()

    @pl.loop(0, LEVELS // 2)
    def _(l):
        local_field(l)

    sub, lane = iota(tile, 0), iota(tile, 1)
    level_of = (lane // 8) % LEVELS
    along_lanes = level_of * POLES + lane % POLES
    along_subs = level_of * POLES + sub % POLES

    def spread(ref, where_to):
        value = jnp.zeros(tile, f32)
        for n in range(LEVELS * POLES):
            value = jnp.where(where_to == n, ref[n // POLES, n % POLES], value)
        return value

    px_l, wx_l = spread(px, along_lanes), spread(wx, along_lanes)
    qx_l = 1.0 - px_l
    corner_decay_x = jnp.exp(log_of(qx_l) * BLOCK)
    square = (128, 128)
    stack = lambda t: jnp.concatenate([t] * 16, axis=0)
    p_c, q_c, g_c = stack(px_l), stack(qx_l), stack(wx_l * jnp.sqrt(1.0 - px_l * px_l))
    p_r, q_r, g_r = p_c.T, q_c.T, g_c.T
    row_id, lane_id = iota(square, 0), iota(square, 1)
    pair = (row_id // 8 == lane_id // 8) & (row_id % 8 < POLES) & (lane_id % 8 >= POLES)
    part = jnp.where(pair, g_r / (q_r + q_c - q_r * q_c), 0.0)
    total = jnp.sum(part, axis=0, keepdims=True)
    total = jnp.where(total > 0.0, total, 1.0)
    corner_mix_x = -(part * p_r) / total

    py_s, wy_s = spread(py, along_subs), spread(wy, along_subs)
    qy_s = 1.0 - py_s
    rate_y = log_of(qy_s)
    slab_decay_y, corner_decay_y = jnp.exp(rate_y * BLOCK), jnp.exp(rate_y * (2 * BLOCK))
    gy_s = wy_s * jnp.sqrt(1.0 - py_s * py_s)
    corner_mix_y, total = [], jnp.zeros(tile, f32)
    for k in range(POLES):
        row = lambda t: jnp.broadcast_to(t[k : k + 1, :], tile)
        q_k = row(qy_s)
        part = row(gy_s) / (qy_s + q_k - qy_s * q_k)
        total += part
        corner_mix_y.append(part * row(py_s))
    corner_mix_y = [-part / total for part in corner_mix_y]

    mix_x, rate_own = end_mix(px, wx, r // 2, (8, BLOCK))
    decay_own_x = jnp.exp(rate_own * BLOCK)
    mix_y, rate_own = end_mix(py, wy, c // 2, tile)
    decay_own_y = jnp.exp(rate_own * (2 * BLOCK))

    @pl.loop(1, PEERS)
    def _(j):
        peer = lax.rem(r + j, PEERS)
        row_copy(peer, peer, *row1).wait_recv()

    entering = scan_blocks([row_in[i, :, 0:256] for i in range(PEERS)], decay_own_x, mix_x)
    for i in range(PEERS):
        row_out2[i] = entering[i]

    @pl.loop(1, PEERS)
    def _(j):
        row_copy(lax.rem(r + j, PEERS), r, *row2).start()

    row_in2[r] = row_out2[r]

    mine = jnp.full(tile, r, jnp.int32)
    corners = [row_in[i, :, 256:384] for i in range(PEERS)]
    state, enter_f = jnp.zeros(tile, f32), jnp.zeros(tile, f32)
    for i in range(PEERS):
        enter_f = jnp.where(mine == i, state, enter_f)
        state = corner_decay_x * state + corners[i]
    state = lax.dot_general(state, corner_mix_x, NN, precision=lax.Precision.HIGHEST, preferred_element_type=f32)
    enter_b = jnp.zeros(tile, f32)
    for i in range(PEERS - 1, -1, -1):
        enter_b = jnp.where(mine == i, state, enter_b)
        state = corner_decay_x * state + corners[i]
    corner = jnp.where(lane % 8 < POLES, enter_f, enter_b)
    swapped = pltpu.roll(corner, 64, 1)
    first = jnp.where(lane < 64, corner, swapped)
    second = jnp.where(lane < 64, swapped, corner)
    forward = sub < POLES
    both = jnp.where(forward, slab_decay_y * first + second, first + slab_decay_y * second)

    @pl.loop(1, PEERS)
    def _(j):
        peer = lax.rem(c + j, PEERS)
        col_copy(peer, peer, *col1).wait_recv()

    entering = scan_blocks([col_in[i] for i in range(PEERS)], decay_own_y, mix_y)
    for i in range(PEERS):
        col_out2[i, 0:8, :] = entering[i]
        col_out2[i, 8:16, :] = both

    @pl.loop(1, PEERS)
    def _(j):
        col_copy(lax.rem(c + j, PEERS), c, *col2).start()

    col_in2[c] = col_out2[c]

    @pl.loop(LEVELS // 2, LEVELS)
    def _(l):
        local_field(l)

    @pl.loop(1, PEERS)
    def _(j):
        peer = lax.rem(c + j, PEERS)
        col_copy(peer, peer, *col2).wait_recv()

    mine = jnp.full(tile, c, jnp.int32)
    corners = [col_in2[i, 8:16, :] for i in range(PEERS)]
    state, enter_f = jnp.zeros(tile, f32), jnp.zeros(tile, f32)
    for i in range(PEERS):
        enter_f = jnp.where(mine == i, state, enter_f)
        state = corner_decay_y * state + corners[i]
    end = jnp.zeros(tile, f32)
    for k in range(POLES):
        end += corner_mix_y[k] * jnp.broadcast_to(state[k : k + 1, :], tile)
    state, enter_b = end, jnp.zeros(tile, f32)
    for i in range(PEERS - 1, -1, -1):
        enter_b = jnp.where(mine == i, state, enter_b)
        state = corner_decay_y * state + corners[i]
    corner_f = jnp.where(lane < 64, enter_f, slab_decay_y * enter_f + first)
    corner_b = jnp.where(lane < 64, slab_decay_y * enter_b + second, enter_b)
    corner = jnp.where(forward, corner_f, corner_b)

    spread_out = jnp.where(row_id // 8 == lane_id // 8, stack(corner), 0.0)
    k_h, k_l = halves(spread_out)
    ex_all = ex_v[...].reshape(64, BLOCK)
    x_h, x_l = halves(jnp.concatenate([ex_all, ex_all], axis=0))
    through = mm(k_h, x_h) + (mm(k_l, x_h) + mm(k_h, x_l))

    @pl.loop(1, PEERS)
    def _(j):
        peer = lax.rem(r + j, PEERS)
        row_copy(peer, peer, *row2).wait_recv()

    rounded = lambda t: t.astype(bf16).astype(f32)
    for l in range(LEVELS):
        decay = jnp.concatenate([decay_y[l], decay_y[l]], axis=1)
        enter = jnp.concatenate([col_in2[2 * l, 0:8, :], col_in2[2 * l + 1, 0:8, :]], axis=1)
        ys = ys_v[l]
        slabs = (
            jnp.where(forward_wide, enter, decay * enter + ys[8:16]),
            jnp.where(forward_wide, decay * enter + ys[0:8], enter),
        )
        x_h = rounded(ex_v[l])
        x_l = ex_v[l] - x_h
        y_h = rounded(ey_v[l])
        y_l = ey_v[l] - y_h
        for s in range(2):
            f = row_in2[2 * l + s]
            f_h = rounded(f)
            f_l = f - f_h
            at = 8 * (s * LEVELS + l)
            g = slabs[s] + through[at : at + 8]
            g_h = rounded(g)
            g_l = g - g_h
            left_out[2 * l + s] = jnp.concatenate([f_h, f_l, f_h, y_h, y_h, y_l], axis=0).astype(bf16)
            right_out[2 * l + s] = jnp.concatenate([x_h, x_h, x_l, g_h, g_l, g_h], axis=0).astype(bf16)

    @pl.loop(1, PEERS)
    def _(j):
        for peer, there, ends, make in (
            (lax.rem(r + j, PEERS), r, row1, row_copy), (lax.rem(r + j, PEERS), r, row2, row_copy),
            (lax.rem(c + j, PEERS), c, col1, col_copy), (lax.rem(c + j, PEERS), c, col2, col_copy),
        ):
            make(peer, there, *ends).wait_send()

    @pl.loop(0, LEVELS)
    def _(l):
        save(l).wait()


def kernel_field(p_ref, left_ref, right_ref, out_ref):
    for s in range(2):
        rows = slice(BLOCK * s, BLOCK * (s + 1))
        out_ref[0, rows, :] = jnp.exp(p_ref[0, rows, :] + mm(left_ref[s], right_ref[s], TN))


def on_device(source, pole_x, weight_x, pole_y, weight_y):
    smem = pl.BlockSpec(memory_space=pltpu.SMEM)
    vmem = pl.BlockSpec(memory_space=pltpu.VMEM)
    hbm = pl.BlockSpec(memory_space=pl.ANY)
    shape = source.shape
    V = pltpu.VMEM
    sems = pltpu.SemaphoreType.DMA((PEERS,))
    local, left, right = pl.pallas_call(
        kernel_states,
        out_shape=(
            jax.ShapeDtypeStruct(shape, f32),
            jax.ShapeDtypeStruct((16, 48, BLOCK), bf16),
            jax.ShapeDtypeStruct((16, 48, BLOCK), bf16),
        ),
        in_specs=[smem] * 4 + [hbm],
        out_specs=(hbm, vmem, vmem),
        scratch_shapes=[
            V(shape, f32), V(shape, bf16), V(shape, bf16),
            V((LEVELS, 528, BLOCK), bf16), V((LEVELS, BLOCK, BLOCK), bf16), V((LEVELS, BLOCK, BLOCK), bf16),
            V((LEVELS, 16, BLOCK), bf16), V((64, BLOCK), f32), V((64, BLOCK), f32),
            V((LEVELS, 8, BLOCK), f32), V((LEVELS, 8, BLOCK), f32), V((LEVELS, 8, 128), f32),
            V((16, 8, BLOCK), f32), V((LEVELS, 16, BLOCK), f32),
            V((PEERS, 8, 384), f32), V((PEERS, 8, 384), f32), V((PEERS, 8, 128), f32), V((PEERS, 8, 128), f32),
            V((PEERS, 8, BLOCK), f32), V((PEERS, 8, BLOCK), f32), V((PEERS, 16, 128), f32), V((PEERS, 16, 128), f32),
            pltpu.SemaphoreType.DMA((LEVELS,)), pltpu.SemaphoreType.DMA((LEVELS,)),
        ] + [sems] * 8,
        compiler_params=pltpu.CompilerParams(collective_id=0, has_side_effects=True, vmem_limit_bytes=48 * 2**20),
    )(pole_x, weight_x, pole_y, weight_y, source)
    field = pl.BlockSpec((1, 2 * BLOCK, BLOCK), lambda l: (l, 0, 0))
    ends = pl.BlockSpec((2, 48, BLOCK), lambda l: (l, 0, 0))
    return pl.pallas_call(
        kernel_field,
        out_shape=jax.ShapeDtypeStruct(shape, f32),
        grid=(LEVELS,),
        in_specs=[field, ends, ends],
        out_specs=field,
    )(local, left, right)


def solution(mesh):
    return jax.shard_map(
        on_device,
        mesh=mesh,
        in_specs=(P(None, "col", "row"), P(), P(), P(), P()),
        out_specs=P(None, "col", "row"),
        check_vma=False,
    )
```

```python
import functools

import jax
import jax.numpy as jnp
from jax import lax
from jax.experimental import pallas as pl
from jax.experimental.pallas import tpu as pltpu
from jax.sharding import PartitionSpec as P

MESH = pl.DeviceIdType.MESH
LEVELS = 8
POLES = 4
BLOCK = 256
PEERS = 16
GROUPS = ((0, 1, 2, 3), (4, 5, 6, 7))
f32 = jnp.float32
bf16 = jnp.bfloat16
NN = (((1,), (0,)), ((), ()))
NT = (((1,), (1,)), ((), ()))
TN = (((0,), (0,)), ((), ()))


def mm(a, b, dims=NN):
    return lax.dot_general(a, b, dims, preferred_element_type=f32)


def halves(value):
    high = value.astype(bf16)
    return high, (value - high.astype(f32)).astype(bf16)


def iota(shape, dim):
    return lax.broadcasted_iota(jnp.int32, shape, dim)


def log_of(short):
    total = jnp.full_like(short, 1.0 / 7.0)
    for n in (6, 5, 4, 3, 2, 1):
        total = total * short + 1.0 / n
    return -short * total


def by_pole(ref, level, shape):
    place = iota(shape, 0) % POLES
    value = jnp.full(shape, ref[POLES - 1, level], f32)
    for k in range(POLES - 1):
        value = jnp.where(place == k, ref[k, level], value)
    return value


def couplings(short, decay, weight, shift):
    gain = jnp.sqrt(1.0 - decay * decay)
    forward, backward = weight * gain, weight * short
    sum_f = jnp.zeros_like(short)
    sum_b = jnp.zeros_like(short)
    for m in range(POLES):
        short_m, f_m, b_m = (short, forward, backward) if m == 0 else tuple(shift(t, m) for t in (short, forward, backward))
        share = 1.0 / (short + short_m - short * short_m)
        sum_f += b_m * share
        sum_b += f_m * share
    return forward, sum_b, forward * sum_f, backward * sum_b


def line_tables(pole_ref, weight_ref, level):
    shape = (8, 128)
    decay, weight = by_pole(pole_ref, level, shape), by_pole(weight_ref, level, shape)
    short = 1.0 - decay
    rate = log_of(short)
    _, _, c_f, c_b = couplings(short, decay, weight, lambda t, m: pltpu.roll(t, m, 0))
    forward = iota((8, BLOCK), 0) < POLES
    place = iota((8, BLOCK), 1)
    wide = lambda t: jnp.concatenate([t, t], axis=1)
    summary = jnp.exp(wide(rate) * jnp.where(forward, BLOCK - 1 - place, place).astype(f32))
    entry = jnp.exp(wide(rate) * jnp.where(forward, place + 1, BLOCK - place).astype(f32))
    entry = entry * jnp.where(forward, wide(c_f), wide(c_b))
    return rate, c_f, c_b, summary, entry


def toeplitz(rate, low, up, store):
    shape = (8, 128)
    sub, lane = iota(shape, 0), iota(shape, 1)
    apart = (sub - lane).astype(f32)
    rates = [jnp.broadcast_to(rate[k : k + 1, :], shape) for k in range(POLES)]
    step = [jnp.exp(8.0 * r) for r in rates]
    below = [jnp.broadcast_to(low[k : k + 1, :], shape) * jnp.exp(rates[k] * apart) for k in range(POLES)]
    above = [jnp.broadcast_to(up[k : k + 1, :], shape) * jnp.exp(rates[k] * (-120.0 - apart)) for k in range(POLES)]
    upper = {}
    for m in range(15, -17, -1):
        upper[m] = (above[0] + above[1]) + (above[2] + above[3])
        above = [a * s for a, s in zip(above, step)]
    tiles = {}
    for m in range(-16, 32):
        if m < 0:
            tiles[m] = upper[m]
            continue
        lower = (below[0] + below[1]) + (below[2] + below[3])
        below = [b * s for b, s in zip(below, step)]
        tiles[m] = lower if m > 15 else jnp.where(sub + 8 * m >= lane, lower, upper[m])
    for m in range(-16, 32, 2):
        high, low_part = halves(jnp.concatenate([tiles[m], tiles[m + 1]], axis=0))
        for j in range(2):
            if 0 <= m + 16 * j < 32:
                store(8 * (m + 16 * j), 128 * j, high, low_part)


def end_mix(pole_ref, weight_ref, level, shape):
    decay, weight = by_pole(pole_ref, level, shape), by_pole(weight_ref, level, shape)
    short = 1.0 - decay
    parts, total = [], jnp.zeros(shape, f32)
    for k in range(POLES):
        p_k = jnp.full(shape, pole_ref[k, level], f32)
        q_k = 1.0 - p_k
        part = weight_ref[k, level] * jnp.sqrt(1.0 - p_k * p_k) / (short + q_k - short * q_k)
        total += part
        parts.append(part * p_k)
    return [-part / total for part in parts], log_of(short)


def scan_blocks(inputs, decay, mix):
    forward = iota(decay.shape, 0) < POLES
    state = jnp.zeros_like(decay)
    before = []
    for block in inputs:
        before.append(state)
        state = decay * state + block
    end = jnp.zeros_like(decay)
    for k in range(POLES):
        end += mix[k] * jnp.broadcast_to(state[k : k + 1, :], decay.shape)
    state = end
    out = [None] * len(inputs)
    for i in range(len(inputs) - 1, -1, -1):
        out[i] = jnp.where(forward, before[i], state)
        state = decay * state + inputs[i]
    return out


def kernel_states(
    px_hbm, wx_hbm, py_hbm, wy_hbm, u_hbm, p_out, left_out, right_out,
    px, wx, py, wy, u_v, zh_v, zl_v, ty_v, txh_v, txl_v, sx_v, sxh_v, sxl_v, ex_v, ey_v, decay_y, v_v,
    row_out, row_in, col_out, col_in, row_out2, row_in2, col_out2, col_in2,
    table_sem, load_sem, row_send, row_recv, col_send, col_recv, row_send2, row_recv2, col_send2, col_recv2,
):
    r, c = lax.axis_index("row"), lax.axis_index("col")
    load = lambda l: pltpu.make_async_copy(u_hbm.at[l], u_v.at[l], load_sem.at[l])

    tables = [
        pltpu.make_async_copy(src, dst, table_sem.at[n])
        for n, (src, dst) in enumerate(((px_hbm, px), (wx_hbm, wx), (py_hbm, py), (wy_hbm, wy)))
    ]
    for table in tables:
        table.start()

    @pl.loop(0, LEVELS)
    def _(l):
        load(l).start()

    barrier = pltpu.get_barrier_semaphore()

    @pl.loop(1, PEERS)
    def _(j):
        pl.semaphore_signal(barrier, inc=1, device_id=(lax.rem(r + j, PEERS), c), device_id_type=MESH)
        pl.semaphore_signal(barrier, inc=1, device_id=(r, lax.rem(c + j, PEERS)), device_id_type=MESH)

    tile = (8, 128)
    for table in tables:
        table.wait()

    toeplitz_x = []
    for l in range(LEVELS):
        rate, c_f, c_b, summary, entry = line_tables(px, wx, l)
        s_h, s_l = halves(summary)
        sx_v[l] = jnp.concatenate([s_h.astype(f32), s_l.astype(f32)], axis=0).astype(bf16)
        sxh_v[pl.ds(8 * l, 8), :] = s_h.astype(f32)
        sxl_v[pl.ds(8 * l, 8), :] = s_l.astype(f32)
        ex_v[l] = entry
        toeplitz_x.append((rate, c_b, c_f))

        rate, c_f, c_b, summary, entry = line_tables(py, wy, l)
        s_h, s_l = halves(summary)
        ty_v[l, 256:272, :] = jnp.concatenate([s_h.astype(f32), s_l.astype(f32)], axis=0).astype(bf16)
        ey_v[l] = entry
        decay_y[l] = jnp.exp(rate * BLOCK)

        def store_y(row, lane, high, low):
            ty_v[l, row : row + 16, lane : lane + 128] = high
            ty_v[l, row + 272 : row + 288, lane : lane + 128] = low

        toeplitz(rate, c_f, c_b, store_y)

    forward_wide = iota((8, BLOCK), 0) < POLES

    def column_products(l):
        sums = []
        for s in range(2):
            rows = slice(BLOCK * s, BLOCK * (s + 1))
            u_h, u_l = halves(u_v[l, rows, :])
            d1 = mm(ty_v[l], u_h)
            d2 = mm(ty_v[l, 0:272, :], u_l)
            z = d1[0:256] + d1[272:528] + d2[0:256]
            v = d1[256:264] + d1[264:272] + d2[256:264]
            z_h, z_l = halves(z)
            zh_v[l, rows, :] = z_h
            zl_v[l, rows, :] = z_l
            v_v[s * LEVELS + l] = v
            sums.append(v)
        decay = jnp.concatenate([decay_y[l], decay_y[l]], axis=1)
        both = jnp.where(forward_wide, decay * sums[0] + sums[1], sums[0] + decay * sums[1])
        col_out[2 * l] = both[:, 0:128]
        col_out[2 * l + 1] = both[:, 128:256]

    def row_states(l):
        for s in range(2):
            rows = slice(BLOCK * s, BLOCK * (s + 1))
            e1 = mm(sx_v[l], zh_v[l, rows, :], NT)
            e2 = mm(sx_v[l], zl_v[l, rows, :], NT)
            row_out[2 * l + s, :, 0:256] = e1[0:8] + e1[8:16] + e2[0:8]

    ready = []
    for group in GROUPS:
        for l in group:
            load(l).wait()
        for l in group:
            column_products(l)
        for l in ready:
            row_states(l)
        ready = group
    for l in ready:
        row_states(l)

    v_h, v_l = halves(v_v[...].reshape(128, BLOCK))
    sxh = jnp.concatenate([sxh_v[...], sxh_v[...]], axis=0).astype(bf16)
    sxl = jnp.concatenate([sxl_v[...], sxl_v[...]], axis=0).astype(bf16)
    corner = mm(v_h, sxh, NT) + (mm(v_l, sxh, NT) + mm(v_h, sxl, NT))
    own = iota((128, 128), 0) // 8 == iota((128, 128), 1) // 8
    corner = jnp.sum(jnp.where(own, corner, 0.0).reshape(16, 8, 128), axis=0)

    @pl.loop(0, PEERS)
    def _(q):
        row_out[q, :, 256:384] = corner

    pl.semaphore_wait(barrier, 2 * (PEERS - 1))

    def row_copy(peer, there, src, dst, send, recv):
        return pltpu.make_async_remote_copy(
            src_ref=src.at[peer], dst_ref=dst.at[there], send_sem=send.at[peer], recv_sem=recv.at[there],
            device_id=(peer, c), device_id_type=MESH,
        )

    def col_copy(peer, there, src, dst, send, recv):
        return pltpu.make_async_remote_copy(
            src_ref=src.at[peer], dst_ref=dst.at[there], send_sem=send.at[peer], recv_sem=recv.at[there],
            device_id=(r, peer), device_id_type=MESH,
        )

    row1 = (row_out, row_in, row_send, row_recv)
    col1 = (col_out, col_in, col_send, col_recv)
    row2 = (row_out2, row_in2, row_send2, row_recv2)
    col2 = (col_out2, col_in2, col_send2, col_recv2)

    @pl.loop(1, PEERS)
    def _(j):
        row_copy(lax.rem(r + j, PEERS), r, *row1).start()
        col_copy(lax.rem(c + j, PEERS), c, *col1).start()

    row_in[r] = row_out[r]
    col_in[c] = col_out[c]

    for l in range(LEVELS):

        def store_x(row, lane, high, low):
            txh_v[l, row : row + 16, lane : lane + 128] = high
            txl_v[l, row : row + 16, lane : lane + 128] = low

        toeplitz(*toeplitz_x[l], store_x)

    def local_field(l):
        p = mm(zh_v[l], txh_v[l]) + (mm(zl_v[l], txh_v[l]) + mm(zh_v[l], txl_v[l]))
        p_out[l] = p

    for l in range(LEVELS // 2):
        local_field(l)

    sub, lane = iota(tile, 0), iota(tile, 1)
    level_of = (lane // 8) % LEVELS
    along_lanes = level_of * POLES + lane % POLES
    along_subs = level_of * POLES + sub % POLES

    def spread(ref, where_to):
        value = jnp.zeros(tile, f32)
        for n in range(LEVELS * POLES):
            value = jnp.where(where_to == n, ref[n % POLES, n // POLES], value)
        return value

    px_l, wx_l = spread(px, along_lanes), spread(wx, along_lanes)
    qx_l = 1.0 - px_l
    corner_decay_x = jnp.exp(log_of(qx_l) * BLOCK)
    square = (128, 128)
    stack = lambda t: jnp.concatenate([t] * 16, axis=0)
    p_c, q_c, g_c = stack(px_l), stack(qx_l), stack(wx_l * jnp.sqrt(1.0 - px_l * px_l))
    p_r, q_r, g_r = p_c.T, q_c.T, g_c.T
    row_id, lane_id = iota(square, 0), iota(square, 1)
    pair = (row_id // 8 == lane_id // 8) & (row_id % 8 < POLES) & (lane_id % 8 >= POLES)
    part = jnp.where(pair, g_r / (q_r + q_c - q_r * q_c), 0.0)
    total = jnp.sum(part, axis=0, keepdims=True)
    total = jnp.where(total > 0.0, total, 1.0)
    corner_mix_x = -(part * p_r) / total

    py_s, wy_s = spread(py, along_subs), spread(wy, along_subs)
    qy_s = 1.0 - py_s
    rate_y = log_of(qy_s)
    slab_decay_y, corner_decay_y = jnp.exp(rate_y * BLOCK), jnp.exp(rate_y * (2 * BLOCK))
    gy_s = wy_s * jnp.sqrt(1.0 - py_s * py_s)
    corner_mix_y, total = [], jnp.zeros(tile, f32)
    for k in range(POLES):
        row = lambda t: jnp.broadcast_to(t[k : k + 1, :], tile)
        q_k = row(qy_s)
        part = row(gy_s) / (qy_s + q_k - qy_s * q_k)
        total += part
        corner_mix_y.append(part * row(py_s))
    corner_mix_y = [-part / total for part in corner_mix_y]

    mix_x, rate_own = end_mix(px, wx, r // 2, (8, BLOCK))
    decay_own_x = jnp.exp(rate_own * BLOCK)
    mix_y, rate_own = end_mix(py, wy, c // 2, tile)
    decay_own_y = jnp.exp(rate_own * (2 * BLOCK))

    @pl.loop(1, PEERS)
    def _(j):
        peer = lax.rem(r + j, PEERS)
        row_copy(peer, peer, *row1).wait_recv()

    entering = scan_blocks([row_in[i, :, 0:256] for i in range(PEERS)], decay_own_x, mix_x)
    for i in range(PEERS):
        row_out2[i] = entering[i]

    @pl.loop(1, PEERS)
    def _(j):
        row_copy(lax.rem(r + j, PEERS), r, *row2).start()

    row_in2[r] = row_out2[r]

    mine = jnp.full(tile, r, jnp.int32)
    corners = [row_in[i, :, 256:384] for i in range(PEERS)]
    state, enter_f = jnp.zeros(tile, f32), jnp.zeros(tile, f32)
    for i in range(PEERS):
        enter_f = jnp.where(mine == i, state, enter_f)
        state = corner_decay_x * state + corners[i]
    state = lax.dot_general(state, corner_mix_x, NN, precision=lax.Precision.HIGHEST, preferred_element_type=f32)
    enter_b = jnp.zeros(tile, f32)
    for i in range(PEERS - 1, -1, -1):
        enter_b = jnp.where(mine == i, state, enter_b)
        state = corner_decay_x * state + corners[i]
    corner = jnp.where(lane % 8 < POLES, enter_f, enter_b)
    swapped = pltpu.roll(corner, 64, 1)
    first = jnp.where(lane < 64, corner, swapped)
    second = jnp.where(lane < 64, swapped, corner)
    forward = sub < POLES
    both = jnp.where(forward, slab_decay_y * first + second, first + slab_decay_y * second)

    @pl.loop(1, PEERS)
    def _(j):
        peer = lax.rem(c + j, PEERS)
        col_copy(peer, peer, *col1).wait_recv()

    entering = scan_blocks([col_in[i] for i in range(PEERS)], decay_own_y, mix_y)
    for i in range(PEERS):
        col_out2[i, 0:8, :] = entering[i]
        col_out2[i, 8:16, :] = both

    @pl.loop(1, PEERS)
    def _(j):
        col_copy(lax.rem(c + j, PEERS), c, *col2).start()

    col_in2[c] = col_out2[c]

    for l in range(LEVELS // 2, LEVELS):
        local_field(l)

    @pl.loop(1, PEERS)
    def _(j):
        peer = lax.rem(c + j, PEERS)
        col_copy(peer, peer, *col2).wait_recv()

    mine = jnp.full(tile, c, jnp.int32)
    corners = [col_in2[i, 8:16, :] for i in range(PEERS)]
    state, enter_f = jnp.zeros(tile, f32), jnp.zeros(tile, f32)
    for i in range(PEERS):
        enter_f = jnp.where(mine == i, state, enter_f)
        state = corner_decay_y * state + corners[i]
    end = jnp.zeros(tile, f32)
    for k in range(POLES):
        end += corner_mix_y[k] * jnp.broadcast_to(state[k : k + 1, :], tile)
    state, enter_b = end, jnp.zeros(tile, f32)
    for i in range(PEERS - 1, -1, -1):
        enter_b = jnp.where(mine == i, state, enter_b)
        state = corner_decay_y * state + corners[i]
    corner_f = jnp.where(lane < 64, enter_f, slab_decay_y * enter_f + first)
    corner_b = jnp.where(lane < 64, slab_decay_y * enter_b + second, enter_b)
    corner = jnp.where(forward, corner_f, corner_b)

    spread_out = jnp.where(row_id // 8 == lane_id // 8, stack(corner), 0.0)
    k_h, k_l = halves(spread_out)
    ex_all = ex_v[...].reshape(64, BLOCK)
    x_h, x_l = halves(jnp.concatenate([ex_all, ex_all], axis=0))
    through = mm(k_h, x_h) + (mm(k_l, x_h) + mm(k_h, x_l))

    @pl.loop(1, PEERS)
    def _(j):
        peer = lax.rem(r + j, PEERS)
        row_copy(peer, peer, *row2).wait_recv()

    rounded = lambda t: t.astype(bf16).astype(f32)
    for l in range(LEVELS):
        decay = jnp.concatenate([decay_y[l], decay_y[l]], axis=1)
        enter = jnp.concatenate([col_in2[2 * l, 0:8, :], col_in2[2 * l + 1, 0:8, :]], axis=1)
        slabs = (
            jnp.where(forward_wide, enter, decay * enter + v_v[LEVELS + l]),
            jnp.where(forward_wide, decay * enter + v_v[l], enter),
        )
        e_h, e_l = halves(jnp.concatenate(slabs, axis=0))
        wide = mm(jnp.concatenate([e_h, e_l], axis=0), txh_v[l])
        wide = wide[0:16] + wide[16:32] + mm(e_h, txl_v[l])
        x_h = rounded(ex_v[l])
        x_l = ex_v[l] - x_h
        y_h = rounded(ey_v[l])
        y_l = ey_v[l] - y_h
        for s in range(2):
            f = row_in2[2 * l + s]
            f_h = rounded(f)
            f_l = f - f_h
            at = 8 * (s * LEVELS + l)
            g = wide[8 * s : 8 * s + 8] + through[at : at + 8]
            g_h = rounded(g)
            g_l = g - g_h
            left_out[2 * l + s] = jnp.concatenate([f_h, f_l, f_h, y_h, y_h, y_l], axis=0).astype(bf16)
            right_out[2 * l + s] = jnp.concatenate([x_h, x_h, x_l, g_h, g_l, g_h], axis=0).astype(bf16)

    @pl.loop(1, PEERS)
    def _(j):
        for peer, there, ends, make in (
            (lax.rem(r + j, PEERS), r, row1, row_copy), (lax.rem(r + j, PEERS), r, row2, row_copy),
            (lax.rem(c + j, PEERS), c, col1, col_copy), (lax.rem(c + j, PEERS), c, col2, col_copy),
        ):
            make(peer, there, *ends).wait_send()


def kernel_field(p_ref, left_ref, right_ref, out_hbm, out_v, save_sem):
    save = lambda l: pltpu.make_async_copy(out_v.at[l], out_hbm.at[l], save_sem.at[l])

    for l in range(LEVELS):
        for s in range(2):
            rows = slice(BLOCK * s, BLOCK * (s + 1))
            out_v[l, rows, :] = jnp.exp(p_ref[l, rows, :] + mm(left_ref[2 * l + s], right_ref[2 * l + s], TN))
        save(l).start()

    @pl.loop(0, LEVELS)
    def _(l):
        save(l).wait()


def on_device(source, pole_x, weight_x, pole_y, weight_y):
    vmem = pl.BlockSpec(memory_space=pltpu.VMEM)
    hbm = pl.BlockSpec(memory_space=pltpu.HBM)
    shape = source.shape
    V = pltpu.VMEM
    sems = pltpu.SemaphoreType.DMA((PEERS,))
    local, left, right = pl.pallas_call(
        kernel_states,
        out_shape=(
            jax.ShapeDtypeStruct(shape, f32),
            jax.ShapeDtypeStruct((16, 48, BLOCK), bf16),
            jax.ShapeDtypeStruct((16, 48, BLOCK), bf16),
        ),
        in_specs=[hbm] * 5,
        out_specs=(vmem, vmem, vmem),
        scratch_shapes=[pltpu.SMEM((POLES, LEVELS), f32)] * 4 + [
            V(shape, f32), V(shape, bf16), V(shape, bf16),
            V((LEVELS, 528, BLOCK), bf16), V((LEVELS, BLOCK, BLOCK), bf16), V((LEVELS, BLOCK, BLOCK), bf16),
            V((LEVELS, 16, BLOCK), bf16), V((64, BLOCK), f32), V((64, BLOCK), f32),
            V((LEVELS, 8, BLOCK), f32), V((LEVELS, 8, BLOCK), f32), V((LEVELS, 8, 128), f32),
            V((16, 8, BLOCK), f32),
            V((PEERS, 8, 384), f32), V((PEERS, 8, 384), f32), V((PEERS, 8, 128), f32), V((PEERS, 8, 128), f32),
            V((PEERS, 8, BLOCK), f32), V((PEERS, 8, BLOCK), f32), V((PEERS, 16, 128), f32), V((PEERS, 16, 128), f32),
            pltpu.SemaphoreType.DMA((4,)), pltpu.SemaphoreType.DMA((LEVELS,)),
        ] + [sems] * 8,
        compiler_params=pltpu.CompilerParams(collective_id=0, has_side_effects=True, vmem_limit_bytes=48 * 2**20),
    )(*(pltpu.with_memory_space_constraint(t.T, pltpu.HBM) for t in (pole_x, weight_x, pole_y, weight_y)), source)
    return pl.pallas_call(
        kernel_field,
        out_shape=jax.ShapeDtypeStruct(shape, f32),
        in_specs=[vmem] * 3,
        out_specs=hbm,
        scratch_shapes=[V(shape, f32), pltpu.SemaphoreType.DMA((LEVELS,))],
        compiler_params=pltpu.CompilerParams(vmem_limit_bytes=24 * 2**20),
    )(local, left, right)


def solution(mesh):
    return jax.shard_map(
        on_device,
        mesh=mesh,
        in_specs=(P(None, "col", "row"), P(), P(), P(), P()),
        out_specs=P(None, "col", "row"),
        check_vma=False,
    )
```

```python
import functools

import jax
import jax.numpy as jnp
from jax import lax
from jax.experimental import pallas as pl
from jax.experimental.pallas import tpu as pltpu
from jax.sharding import PartitionSpec as P

MESH = pl.DeviceIdType.MESH
LEVELS = 8
POLES = 4
BLOCK = 256
PEERS = 16
EARLY = 2
GROUPS = ((0, 1, 2, 3), (4, 5, 6, 7))
f32 = jnp.float32
bf16 = jnp.bfloat16
NN = (((1,), (0,)), ((), ()))
NT = (((1,), (1,)), ((), ()))
TN = (((0,), (0,)), ((), ()))


def mm(a, b, dims=NN):
    return lax.dot_general(a, b, dims, preferred_element_type=f32)


def halves(value):
    high = value.astype(bf16)
    return high, (value - high.astype(f32)).astype(bf16)


def iota(shape, dim):
    return lax.broadcasted_iota(jnp.int32, shape, dim)


def log_of(short):
    total = jnp.full_like(short, 1.0 / 7.0)
    for n in (6, 5, 4, 3, 2, 1):
        total = total * short + 1.0 / n
    return -short * total


def by_pole(ref, level, shape):
    place = iota(shape, 0) % POLES
    value = jnp.full(shape, ref[POLES - 1, level], f32)
    for k in range(POLES - 1):
        value = jnp.where(place == k, ref[k, level], value)
    return value


def couplings(short, decay, weight, shift):
    gain = jnp.sqrt(1.0 - decay * decay)
    forward, backward = weight * gain, weight * short
    sum_f = jnp.zeros_like(short)
    sum_b = jnp.zeros_like(short)
    for m in range(POLES):
        short_m, f_m, b_m = (short, forward, backward) if m == 0 else tuple(shift(t, m) for t in (short, forward, backward))
        share = 1.0 / (short + short_m - short * short_m)
        sum_f += b_m * share
        sum_b += f_m * share
    return forward, sum_b, forward * sum_f, backward * sum_b


def line_tables(pole_ref, weight_ref, level):
    shape = (8, 128)
    decay, weight = by_pole(pole_ref, level, shape), by_pole(weight_ref, level, shape)
    short = 1.0 - decay
    rate = log_of(short)
    _, _, c_f, c_b = couplings(short, decay, weight, lambda t, m: pltpu.roll(t, m, 0))
    forward = iota((8, BLOCK), 0) < POLES
    place = iota((8, BLOCK), 1)
    wide = lambda t: jnp.concatenate([t, t], axis=1)
    summary = jnp.exp(wide(rate) * jnp.where(forward, BLOCK - 1 - place, place).astype(f32))
    entry = jnp.exp(wide(rate) * jnp.where(forward, place + 1, BLOCK - place).astype(f32))
    entry = entry * jnp.where(forward, wide(c_f), wide(c_b))
    return rate, c_f, c_b, summary, entry


def toeplitz(rate, low, up, store):
    shape = (8, 128)
    sub, lane = iota(shape, 0), iota(shape, 1)
    apart = (sub - lane).astype(f32)
    rates = [jnp.broadcast_to(rate[k : k + 1, :], shape) for k in range(POLES)]
    step = [jnp.exp(8.0 * r) for r in rates]
    below = [jnp.broadcast_to(low[k : k + 1, :], shape) * jnp.exp(rates[k] * apart) for k in range(POLES)]
    above = [jnp.broadcast_to(up[k : k + 1, :], shape) * jnp.exp(rates[k] * (-120.0 - apart)) for k in range(POLES)]
    upper = {}
    for m in range(15, -17, -1):
        upper[m] = (above[0] + above[1]) + (above[2] + above[3])
        above = [a * s for a, s in zip(above, step)]
    tiles = {}
    for m in range(-16, 32):
        if m < 0:
            tiles[m] = upper[m]
            continue
        lower = (below[0] + below[1]) + (below[2] + below[3])
        below = [b * s for b, s in zip(below, step)]
        tiles[m] = lower if m > 15 else jnp.where(sub + 8 * m >= lane, lower, upper[m])
    for m in range(-16, 32, 2):
        high, low_part = halves(jnp.concatenate([tiles[m], tiles[m + 1]], axis=0))
        for j in range(2):
            if 0 <= m + 16 * j < 32:
                store(8 * (m + 16 * j), 128 * j, high, low_part)


def end_mix(pole_ref, weight_ref, level, shape):
    decay, weight = by_pole(pole_ref, level, shape), by_pole(weight_ref, level, shape)
    short = 1.0 - decay
    parts, total = [], jnp.zeros(shape, f32)
    for k in range(POLES):
        p_k = jnp.full(shape, pole_ref[k, level], f32)
        q_k = 1.0 - p_k
        part = weight_ref[k, level] * jnp.sqrt(1.0 - p_k * p_k) / (short + q_k - short * q_k)
        total += part
        parts.append(part * p_k)
    return [-part / total for part in parts], log_of(short)


def scan_blocks(inputs, decay, mix):
    forward = iota(decay.shape, 0) < POLES
    state = jnp.zeros_like(decay)
    before = []
    for block in inputs:
        before.append(state)
        state = decay * state + block
    end = jnp.zeros_like(decay)
    for k in range(POLES):
        end += mix[k] * jnp.broadcast_to(state[k : k + 1, :], decay.shape)
    state = end
    out = [None] * len(inputs)
    for i in range(len(inputs) - 1, -1, -1):
        out[i] = jnp.where(forward, before[i], state)
        state = decay * state + inputs[i]
    return out


def kernel_states(
    px_hbm, wx_hbm, py_hbm, wy_hbm, u_hbm, p_out, left_out, right_out,
    px, wx, py, wy, u_v, uh_v, ul_v, zh_v, zl_v, ty_v, sy_v, txh_v, txl_v, sx_v, sxh_v, sxl_v, ex_v, ey_v, decay_y, v_v,
    row_out, row_in, col_out, col_in, row_out2, row_in2, col_out2, col_in2,
    table_sem, load_sem, row_send, row_recv, col_send, col_recv, row_send2, row_recv2, col_send2, col_recv2,
):
    r, c = lax.axis_index("row"), lax.axis_index("col")
    load = lambda l: pltpu.make_async_copy(u_hbm.at[l], u_v.at[l], load_sem.at[l])

    tables = [
        pltpu.make_async_copy(src, dst, table_sem.at[n])
        for n, (src, dst) in enumerate(((px_hbm, px), (wx_hbm, wx), (py_hbm, py), (wy_hbm, wy)))
    ]
    for table in tables:
        table.start()

    @pl.loop(0, LEVELS)
    def _(l):
        load(l).start()

    barrier = pltpu.get_barrier_semaphore()

    @pl.loop(1, PEERS)
    def _(j):
        pl.semaphore_signal(barrier, inc=1, device_id=(lax.rem(r + j, PEERS), c), device_id_type=MESH)
        pl.semaphore_signal(barrier, inc=1, device_id=(r, lax.rem(c + j, PEERS)), device_id_type=MESH)

    tile = (8, 128)
    for table in tables:
        table.wait()

    toeplitz_x, toeplitz_y = [], []
    for l in range(LEVELS):
        rate, c_f, c_b, summary, entry = line_tables(px, wx, l)
        s_h, s_l = halves(summary)
        sx_v[l] = jnp.concatenate([s_h.astype(f32), s_l.astype(f32)], axis=0).astype(bf16)
        sxh_v[pl.ds(8 * l, 8), :] = s_h.astype(f32)
        sxl_v[pl.ds(8 * l, 8), :] = s_l.astype(f32)
        ex_v[l] = entry
        toeplitz_x.append((rate, c_b, c_f))

        rate, c_f, c_b, summary, entry = line_tables(py, wy, l)
        s_h, s_l = halves(summary)
        sy_v[l] = jnp.concatenate([s_h.astype(f32), s_l.astype(f32)], axis=0).astype(bf16)
        ey_v[l] = entry
        decay_y[l] = jnp.exp(rate * BLOCK)
        toeplitz_y.append((rate, c_f, c_b))

    forward_wide = iota((8, BLOCK), 0) < POLES

    def column_states(l):
        sums = []
        for s in range(2):
            rows = slice(BLOCK * s, BLOCK * (s + 1))
            u_h, u_l = halves(u_v[l, rows, :])
            uh_v[l, rows, :] = u_h
            ul_v[l, rows, :] = u_l
            d1 = mm(sy_v[l], u_h)
            d2 = mm(sy_v[l], u_l)
            v = d1[0:8] + d1[8:16] + d2[0:8]
            v_v[s * LEVELS + l] = v
            sums.append(v)
        decay = jnp.concatenate([decay_y[l], decay_y[l]], axis=1)
        both = jnp.where(forward_wide, decay * sums[0] + sums[1], sums[0] + decay * sums[1])
        col_out[2 * l] = both[:, 0:128]
        col_out[2 * l + 1] = both[:, 128:256]

    def row_states(l):
        for s in range(2):
            rows = slice(BLOCK * s, BLOCK * (s + 1))
            e1 = mm(sx_v[l], uh_v[l, rows, :], NT)
            e2 = mm(sx_v[l], ul_v[l, rows, :], NT)
            row_out[2 * l + s, :, 0:256] = e1[0:8] + e1[8:16] + e2[0:8]

    for group in GROUPS:
        for l in group:
            load(l).wait()
        for l in group:
            column_states(l)
        for l in group:
            row_states(l)

    v_h, v_l = halves(v_v[...].reshape(128, BLOCK))
    sxh = jnp.concatenate([sxh_v[...], sxh_v[...]], axis=0).astype(bf16)
    sxl = jnp.concatenate([sxl_v[...], sxl_v[...]], axis=0).astype(bf16)
    corner = mm(v_h, sxh, NT) + (mm(v_l, sxh, NT) + mm(v_h, sxl, NT))
    own = iota((128, 128), 0) // 8 == iota((128, 128), 1) // 8
    corner = jnp.sum(jnp.where(own, corner, 0.0).reshape(16, 8, 128), axis=0)

    @pl.loop(0, PEERS)
    def _(q):
        row_out[q, :, 256:384] = corner

    pl.semaphore_wait(barrier, 2 * (PEERS - 1))

    def row_copy(peer, there, src, dst, send, recv):
        return pltpu.make_async_remote_copy(
            src_ref=src.at[peer], dst_ref=dst.at[there], send_sem=send.at[peer], recv_sem=recv.at[there],
            device_id=(peer, c), device_id_type=MESH,
        )

    def col_copy(peer, there, src, dst, send, recv):
        rows = pl.ds(0, 8 if src is col_out else 12)
        return pltpu.make_async_remote_copy(
            src_ref=src.at[peer, rows], dst_ref=dst.at[there, rows], send_sem=send.at[peer], recv_sem=recv.at[there],
            device_id=(r, peer), device_id_type=MESH,
        )

    row1 = (row_out, row_in, row_send, row_recv)
    col1 = (col_out, col_in, col_send, col_recv)
    row2 = (row_out2, row_in2, row_send2, row_recv2)
    col2 = (col_out2, col_in2, col_send2, col_recv2)

    @pl.loop(1, PEERS)
    def _(j):
        row_copy(lax.rem(r + j, PEERS), r, *row1).start()
        col_copy(lax.rem(c + j, PEERS), c, *col1).start()

    row_in[r] = row_out[r]
    col_in[c] = col_out[c]

    for l in range(LEVELS):

        def store_y(row, lane, high, low):
            ty_v[l, row : row + 16, lane : lane + 128] = high
            ty_v[l, row + 256 : row + 272, lane : lane + 128] = low

        def store_x(row, lane, high, low):
            txh_v[l, row : row + 16, lane : lane + 128] = high
            txl_v[l, row : row + 16, lane : lane + 128] = low

        toeplitz(*toeplitz_y[l], store_y)
        toeplitz(*toeplitz_x[l], store_x)

    for l in range(LEVELS):
        for s in range(2):
            rows = slice(BLOCK * s, BLOCK * (s + 1))
            d1 = mm(ty_v[l], uh_v[l, rows, :])
            d2 = mm(ty_v[l, 0:256, :], ul_v[l, rows, :])
            z_h, z_l = halves(d1[0:256] + d1[256:512] + d2)
            zh_v[l, rows, :] = z_h
            zl_v[l, rows, :] = z_l

    def local_field(l):
        p_out[l] = mm(zh_v[l], txh_v[l]) + (mm(zl_v[l], txh_v[l]) + mm(zh_v[l], txl_v[l]))

    for l in range(EARLY):
        local_field(l)

    sub, lane = iota(tile, 0), iota(tile, 1)
    level_of = (lane // 8) % LEVELS
    along_lanes = level_of * POLES + lane % POLES
    along_subs = level_of * POLES + sub % POLES

    def spread(ref, where_to):
        value = jnp.zeros(tile, f32)
        for n in range(LEVELS * POLES):
            value = jnp.where(where_to == n, ref[n % POLES, n // POLES], value)
        return value

    px_l, wx_l = spread(px, along_lanes), spread(wx, along_lanes)
    qx_l = 1.0 - px_l
    corner_decay_x = jnp.exp(log_of(qx_l) * BLOCK)
    square = (128, 128)
    stack = lambda t: jnp.concatenate([t] * 16, axis=0)
    p_c, q_c, g_c = stack(px_l), stack(qx_l), stack(wx_l * jnp.sqrt(1.0 - px_l * px_l))
    p_r, q_r, g_r = p_c.T, q_c.T, g_c.T
    row_id, lane_id = iota(square, 0), iota(square, 1)
    pair = (row_id // 8 == lane_id // 8) & (row_id % 8 < POLES) & (lane_id % 8 >= POLES)
    part = jnp.where(pair, g_r / (q_r + q_c - q_r * q_c), 0.0)
    total = jnp.sum(part, axis=0, keepdims=True)
    total = jnp.where(total > 0.0, total, 1.0)
    corner_mix_x = -(part * p_r) / total

    py_s, wy_s = spread(py, along_subs), spread(wy, along_subs)
    qy_s = 1.0 - py_s
    rate_y = log_of(qy_s)
    slab_decay_y, corner_decay_y = jnp.exp(rate_y * BLOCK), jnp.exp(rate_y * (2 * BLOCK))
    gy_s = wy_s * jnp.sqrt(1.0 - py_s * py_s)
    corner_mix_y, total = [], jnp.zeros(tile, f32)
    for k in range(POLES):
        row = lambda t: jnp.broadcast_to(t[k : k + 1, :], tile)
        q_k = row(qy_s)
        part = row(gy_s) / (qy_s + q_k - qy_s * q_k)
        total += part
        corner_mix_y.append(part * row(py_s))
    corner_mix_y = [-part / total for part in corner_mix_y]

    mix_x, rate_own = end_mix(px, wx, r // 2, (8, BLOCK))
    decay_own_x = jnp.exp(rate_own * BLOCK)
    mix_y, rate_own = end_mix(py, wy, c // 2, tile)
    decay_own_y = jnp.exp(rate_own * (2 * BLOCK))

    @pl.loop(1, PEERS)
    def _(j):
        peer = lax.rem(r + j, PEERS)
        row_copy(peer, peer, *row1).wait_recv()

    entering = scan_blocks([row_in[i, :, 0:256] for i in range(PEERS)], decay_own_x, mix_x)
    f_h, f_l = halves(jnp.concatenate(entering, axis=0))
    high = mm(jnp.concatenate([f_h, f_l], axis=0), ty_v[r // 2, 0:256, :], NT)
    through = high[0:128] + (high[128:256] + mm(f_h, ty_v[r // 2, 256:512, :], NT))
    for i in range(PEERS):
        row_out2[i] = through[8 * i : 8 * i + 8]

    @pl.loop(1, PEERS)
    def _(j):
        row_copy(lax.rem(r + j, PEERS), r, *row2).start()

    row_in2[r] = row_out2[r]

    mine = jnp.full(tile, r, jnp.int32)
    corners = [row_in[i, :, 256:384] for i in range(PEERS)]
    state, enter_f = jnp.zeros(tile, f32), jnp.zeros(tile, f32)
    for i in range(PEERS):
        enter_f = jnp.where(mine == i, state, enter_f)
        state = corner_decay_x * state + corners[i]
    state = lax.dot_general(state, corner_mix_x, NN, precision=lax.Precision.HIGHEST, preferred_element_type=f32)
    enter_b = jnp.zeros(tile, f32)
    for i in range(PEERS - 1, -1, -1):
        enter_b = jnp.where(mine == i, state, enter_b)
        state = corner_decay_x * state + corners[i]
    corner = jnp.where(lane % 8 < POLES, enter_f, enter_b)
    swapped = pltpu.roll(corner, 64, 1)
    first = jnp.where(lane < 64, corner, swapped)
    second = jnp.where(lane < 64, swapped, corner)
    forward = sub < POLES
    both = jnp.where(forward, slab_decay_y * first + second, first + slab_decay_y * second)

    packed = jnp.where(lane < 64, both, pltpu.roll(both, POLES, 0))[0:POLES]

    @pl.loop(1, PEERS)
    def _(j):
        peer = lax.rem(c + j, PEERS)
        col_copy(peer, peer, *col1).wait_recv()

    entering = scan_blocks([col_in[i] for i in range(PEERS)], decay_own_y, mix_y)
    for i in range(PEERS):
        col_out2[i, 0:8, :] = entering[i]
        col_out2[i, 8:12, :] = packed

    @pl.loop(1, PEERS)
    def _(j):
        col_copy(lax.rem(c + j, PEERS), c, *col2).start()

    col_in2[c, 0:12, :] = col_out2[c, 0:12, :]

    for l in range(EARLY, LEVELS):
        local_field(l)

    @pl.loop(1, PEERS)
    def _(j):
        peer = lax.rem(c + j, PEERS)
        col_copy(peer, peer, *col2).wait_recv()

    half = (POLES, 128)
    mine = jnp.full(half, c, jnp.int32)
    corners = [col_in2[i, 8:12, :] for i in range(PEERS)]
    decay = corner_decay_y[0:POLES]
    state, enter_f = jnp.zeros(half, f32), jnp.zeros(half, f32)
    for i in range(PEERS):
        enter_f = jnp.where(mine == i, state, enter_f)
        state = decay * state + corners[i]
    end = jnp.zeros(half, f32)
    for k in range(POLES):
        end += corner_mix_y[k][0:POLES] * jnp.broadcast_to(state[k : k + 1, :], half)
    turn = lambda t: pltpu.roll(jnp.concatenate([t, t], axis=0), 64, 1)
    state, enter_b = turn(end)[0:POLES], jnp.zeros(half, f32)
    for i in range(PEERS - 1, -1, -1):
        enter_b = jnp.where(mine == i, state, enter_b)
        state = decay * state + corners[i]
    twice = lambda t: jnp.concatenate([t, t], axis=0)
    enter_f = jnp.where(lane < 64, twice(enter_f), turn(enter_f))
    enter_b = jnp.where(lane < 64, turn(enter_b), twice(enter_b))
    corner_f = jnp.where(lane < 64, enter_f, slab_decay_y * enter_f + first)
    corner_b = jnp.where(lane < 64, slab_decay_y * enter_b + second, enter_b)
    corner = jnp.where(forward, corner_f, corner_b)

    spread_out = jnp.where(row_id // 8 == lane_id // 8, stack(corner), 0.0)
    k_h, k_l = halves(spread_out)
    ex_all = ex_v[...].reshape(64, BLOCK)
    x_h, x_l = halves(jnp.concatenate([ex_all, ex_all], axis=0))
    through = mm(k_h, x_h) + (mm(k_l, x_h) + mm(k_h, x_l))

    @pl.loop(1, PEERS)
    def _(j):
        peer = lax.rem(r + j, PEERS)
        row_copy(peer, peer, *row2).wait_recv()

    rounded = lambda t: t.astype(bf16).astype(f32)
    for l in range(LEVELS):
        decay = jnp.concatenate([decay_y[l], decay_y[l]], axis=1)
        enter = jnp.concatenate([col_in2[2 * l, 0:8, :], col_in2[2 * l + 1, 0:8, :]], axis=1)
        slabs = (
            jnp.where(forward_wide, enter, decay * enter + v_v[LEVELS + l]),
            jnp.where(forward_wide, decay * enter + v_v[l], enter),
        )
        e_h, e_l = halves(jnp.concatenate(slabs, axis=0))
        wide = mm(jnp.concatenate([e_h, e_l], axis=0), txh_v[l])
        wide = wide[0:16] + wide[16:32] + mm(e_h, txl_v[l])
        x_h = rounded(ex_v[l])
        x_l = ex_v[l] - x_h
        y_h = rounded(ey_v[l])
        y_l = ey_v[l] - y_h
        for s in range(2):
            f = row_in2[2 * l + s]
            f_h = rounded(f)
            f_l = f - f_h
            at = 8 * (s * LEVELS + l)
            g = wide[8 * s : 8 * s + 8] + through[at : at + 8]
            g_h = rounded(g)
            g_l = g - g_h
            left_out[2 * l + s] = jnp.concatenate([f_h, f_l, f_h, y_h, y_h, y_l], axis=0).astype(bf16)
            right_out[2 * l + s] = jnp.concatenate([x_h, x_h, x_l, g_h, g_l, g_h], axis=0).astype(bf16)

    @pl.loop(1, PEERS)
    def _(j):
        for peer, there, ends, make in (
            (lax.rem(r + j, PEERS), r, row1, row_copy), (lax.rem(r + j, PEERS), r, row2, row_copy),
            (lax.rem(c + j, PEERS), c, col1, col_copy), (lax.rem(c + j, PEERS), c, col2, col_copy),
        ):
            make(peer, there, *ends).wait_send()


def kernel_field(p_ref, left_ref, right_ref, out_hbm, out_v, save_sem):
    save = lambda l: pltpu.make_async_copy(out_v.at[l], out_hbm.at[l], save_sem.at[l])

    for l in range(LEVELS):
        for s in range(2):
            rows = slice(BLOCK * s, BLOCK * (s + 1))
            out_v[l, rows, :] = jnp.exp(p_ref[l, rows, :] + mm(left_ref[2 * l + s], right_ref[2 * l + s], TN))
        save(l).start()

    @pl.loop(0, LEVELS)
    def _(l):
        save(l).wait()


def on_device(source, pole_x, weight_x, pole_y, weight_y):
    vmem = pl.BlockSpec(memory_space=pltpu.VMEM)
    hbm = pl.BlockSpec(memory_space=pltpu.HBM)
    shape = source.shape
    V = pltpu.VMEM
    sems = pltpu.SemaphoreType.DMA((PEERS,))
    local, left, right = pl.pallas_call(
        kernel_states,
        out_shape=(
            jax.ShapeDtypeStruct(shape, f32),
            jax.ShapeDtypeStruct((16, 48, BLOCK), bf16),
            jax.ShapeDtypeStruct((16, 48, BLOCK), bf16),
        ),
        in_specs=[hbm] * 5,
        out_specs=(vmem, vmem, vmem),
        scratch_shapes=[pltpu.SMEM((POLES, LEVELS), f32)] * 4 + [
            V(shape, f32), V(shape, bf16), V(shape, bf16), V(shape, bf16), V(shape, bf16),
            V((LEVELS, 512, BLOCK), bf16), V((LEVELS, 16, BLOCK), bf16), V((LEVELS, BLOCK, BLOCK), bf16), V((LEVELS, BLOCK, BLOCK), bf16),
            V((LEVELS, 16, BLOCK), bf16), V((64, BLOCK), f32), V((64, BLOCK), f32),
            V((LEVELS, 8, BLOCK), f32), V((LEVELS, 8, BLOCK), f32), V((LEVELS, 8, 128), f32),
            V((16, 8, BLOCK), f32),
            V((PEERS, 8, 384), f32), V((PEERS, 8, 384), f32), V((PEERS, 8, 128), f32), V((PEERS, 8, 128), f32),
            V((PEERS, 8, BLOCK), f32), V((PEERS, 8, BLOCK), f32), V((PEERS, 16, 128), f32), V((PEERS, 16, 128), f32),
            pltpu.SemaphoreType.DMA((4,)), pltpu.SemaphoreType.DMA((LEVELS,)),
        ] + [sems] * 8,
        compiler_params=pltpu.CompilerParams(collective_id=0, has_side_effects=True, vmem_limit_bytes=48 * 2**20),
    )(*(pltpu.with_memory_space_constraint(t.T, pltpu.HBM) for t in (pole_x, weight_x, pole_y, weight_y)), source)
    return pl.pallas_call(
        kernel_field,
        out_shape=jax.ShapeDtypeStruct(shape, f32),
        in_specs=[vmem] * 3,
        out_specs=hbm,
        scratch_shapes=[V(shape, f32), pltpu.SemaphoreType.DMA((LEVELS,))],
        compiler_params=pltpu.CompilerParams(vmem_limit_bytes=24 * 2**20),
    )(local, left, right)


def solution(mesh):
    return jax.shard_map(
        on_device,
        mesh=mesh,
        in_specs=(P(None, "col", "row"), P(), P(), P(), P()),
        out_specs=P(None, "col", "row"),
        check_vma=False,
    )
```

```python
import functools

import jax
import jax.numpy as jnp
from jax import lax
from jax.experimental import pallas as pl
from jax.experimental.pallas import tpu as pltpu
from jax.sharding import PartitionSpec as P

MESH = pl.DeviceIdType.MESH
LEVELS = 8
POLES = 4
BLOCK = 256
PEERS = 16
EARLY = 2
GROUPS = ((0, 1, 2), (3, 4, 5), (6, 7))
f32 = jnp.float32
bf16 = jnp.bfloat16
NN = (((1,), (0,)), ((), ()))
NT = (((1,), (1,)), ((), ()))
TN = (((0,), (0,)), ((), ()))


def mm(a, b, dims=NN):
    return lax.dot_general(a, b, dims, preferred_element_type=f32)


def halves(value):
    high = value.astype(bf16)
    return high, (value - high.astype(f32)).astype(bf16)


def iota(shape, dim):
    return lax.broadcasted_iota(jnp.int32, shape, dim)


def log_of(short):
    total = jnp.full_like(short, 1.0 / 7.0)
    for n in (6, 5, 4, 3, 2, 1):
        total = total * short + 1.0 / n
    return -short * total


def by_pole(ref, level, shape):
    place = iota(shape, 0) % POLES
    value = jnp.full(shape, ref[POLES - 1, level], f32)
    for k in range(POLES - 1):
        value = jnp.where(place == k, ref[k, level], value)
    return value


def couplings(short, decay, weight, shift):
    gain = jnp.sqrt(1.0 - decay * decay)
    forward, backward = weight * gain, weight * short
    sum_f = jnp.zeros_like(short)
    sum_b = jnp.zeros_like(short)
    for m in range(POLES):
        short_m, f_m, b_m = (short, forward, backward) if m == 0 else tuple(shift(t, m) for t in (short, forward, backward))
        share = 1.0 / (short + short_m - short * short_m)
        sum_f += b_m * share
        sum_b += f_m * share
    return forward, sum_b, forward * sum_f, backward * sum_b


def line_tables(pole_ref, weight_ref, level):
    shape = (8, 128)
    decay, weight = by_pole(pole_ref, level, shape), by_pole(weight_ref, level, shape)
    short = 1.0 - decay
    rate = log_of(short)
    _, _, c_f, c_b = couplings(short, decay, weight, lambda t, m: pltpu.roll(t, m, 0))
    forward = iota((8, BLOCK), 0) < POLES
    place = iota((8, BLOCK), 1)
    wide = lambda t: jnp.concatenate([t, t], axis=1)
    summary = jnp.exp(wide(rate) * jnp.where(forward, BLOCK - 1 - place, place).astype(f32))
    entry = jnp.exp(wide(rate) * jnp.where(forward, place + 1, BLOCK - place).astype(f32))
    entry = entry * jnp.where(forward, wide(c_f), wide(c_b))
    return rate, c_f, c_b, summary, entry


def toeplitz(rate, low, up, store):
    shape = (8, 128)
    sub, lane = iota(shape, 0), iota(shape, 1)
    apart = (sub - lane).astype(f32)
    rates = [jnp.broadcast_to(rate[k : k + 1, :], shape) for k in range(POLES)]
    step = [jnp.exp(8.0 * r) for r in rates]
    below = [jnp.broadcast_to(low[k : k + 1, :], shape) * jnp.exp(rates[k] * apart) for k in range(POLES)]
    above = [jnp.broadcast_to(up[k : k + 1, :], shape) * jnp.exp(rates[k] * (-120.0 - apart)) for k in range(POLES)]
    upper = {}
    for m in range(15, -17, -1):
        upper[m] = (above[0] + above[1]) + (above[2] + above[3])
        above = [a * s for a, s in zip(above, step)]
    tiles = {}
    for m in range(-16, 32):
        if m < 0:
            tiles[m] = upper[m]
            continue
        lower = (below[0] + below[1]) + (below[2] + below[3])
        below = [b * s for b, s in zip(below, step)]
        tiles[m] = lower if m > 15 else jnp.where(sub + 8 * m >= lane, lower, upper[m])
    for m in range(-16, 32, 2):
        high, low_part = halves(jnp.concatenate([tiles[m], tiles[m + 1]], axis=0))
        for j in range(2):
            if 0 <= m + 16 * j < 32:
                store(8 * (m + 16 * j), 128 * j, high, low_part)


def end_mix(pole_ref, weight_ref, level, shape):
    decay, weight = by_pole(pole_ref, level, shape), by_pole(weight_ref, level, shape)
    short = 1.0 - decay
    parts, total = [], jnp.zeros(shape, f32)
    for k in range(POLES):
        p_k = jnp.full(shape, pole_ref[k, level], f32)
        q_k = 1.0 - p_k
        part = weight_ref[k, level] * jnp.sqrt(1.0 - p_k * p_k) / (short + q_k - short * q_k)
        total += part
        parts.append(part * p_k)
    return [-part / total for part in parts], log_of(short)


def scan_blocks(inputs, decay, mix):
    forward = iota(decay.shape, 0) < POLES
    state = jnp.zeros_like(decay)
    before = []
    for block in inputs:
        before.append(state)
        state = decay * state + block
    end = jnp.zeros_like(decay)
    for k in range(POLES):
        end += mix[k] * jnp.broadcast_to(state[k : k + 1, :], decay.shape)
    state = end
    out = [None] * len(inputs)
    for i in range(len(inputs) - 1, -1, -1):
        out[i] = jnp.where(forward, before[i], state)
        state = decay * state + inputs[i]
    return out


def row_peers(r):
    reach = (0, 1, 2, 1)
    steps = [(dx, dy) for dx in range(4) for dy in range(4) if dx or dy]
    steps.sort(key=lambda d: -(reach[d[0]] + reach[d[1]]))
    return [lax.rem(r // 4 + dx, 4) * 4 + lax.rem(lax.rem(r, 4) + dy, 4) for dx, dy in steps]


def col_peers(c):
    steps = [(dz, core) for dz in (4, 3, 5, 2, 6, 1, 7, 0) for core in (0, 1) if dz or core]
    return [lax.rem(c // 2 + dz, 8) * 2 + lax.rem(lax.rem(c, 2) + core, 2) for dz, core in steps]


def kernel_states(
    px_hbm, wx_hbm, py_hbm, wy_hbm, u_hbm, p_out, left_out, right_out,
    px, wx, py, wy, u_v, uh_v, ul_v, zh_v, zl_v, ty_v, sy_v, txh_v, txl_v, sx_v, sxh_v, sxl_v, ex_v, ey_v, decay_y, v_v,
    row_out, row_in, col_out, col_in, row_out2, row_in2, col_out2, col_in2,
    table_sem, load_sem, row_send, row_recv, col_send, col_recv, row_send2, row_recv2, col_send2, col_recv2,
):
    r, c = lax.axis_index("row"), lax.axis_index("col")
    load = lambda l: pltpu.make_async_copy(u_hbm.at[l], u_v.at[l], load_sem.at[l])

    tables = [
        pltpu.make_async_copy(src, dst, table_sem.at[n])
        for n, (src, dst) in enumerate(((px_hbm, px), (wx_hbm, wx), (py_hbm, py), (wy_hbm, wy)))
    ]
    for table in tables:
        table.start()

    @pl.loop(0, LEVELS)
    def _(l):
        load(l).start()

    barrier = pltpu.get_barrier_semaphore()

    @pl.loop(1, PEERS)
    def _(j):
        pl.semaphore_signal(barrier, inc=1, device_id=(lax.rem(r + j, PEERS), c), device_id_type=MESH)
        pl.semaphore_signal(barrier, inc=1, device_id=(r, lax.rem(c + j, PEERS)), device_id_type=MESH)

    tile = (8, 128)
    for table in tables:
        table.wait()

    toeplitz_x, toeplitz_y = [], []
    for l in range(LEVELS):
        rate, c_f, c_b, summary, entry = line_tables(px, wx, l)
        s_h, s_l = halves(summary)
        sx_v[l] = jnp.concatenate([s_h.astype(f32), s_l.astype(f32)], axis=0).astype(bf16)
        sxh_v[pl.ds(8 * l, 8), :] = s_h.astype(f32)
        sxl_v[pl.ds(8 * l, 8), :] = s_l.astype(f32)
        ex_v[l] = entry
        toeplitz_x.append((rate, c_b, c_f))

        rate, c_f, c_b, summary, entry = line_tables(py, wy, l)
        s_h, s_l = halves(summary)
        sy_v[l] = jnp.concatenate([s_h.astype(f32), s_l.astype(f32)], axis=0).astype(bf16)
        ey_v[l] = entry
        decay_y[l] = jnp.exp(rate * BLOCK)
        toeplitz_y.append((rate, c_f, c_b))

    forward_wide = iota((8, BLOCK), 0) < POLES

    def column_states(l):
        sums = []
        for s in range(2):
            rows = slice(BLOCK * s, BLOCK * (s + 1))
            u_h, u_l = halves(u_v[l, rows, :])
            uh_v[l, rows, :] = u_h
            ul_v[l, rows, :] = u_l
            d1 = mm(sy_v[l], u_h)
            d2 = mm(sy_v[l], u_l)
            v = d1[0:8] + d1[8:16] + d2[0:8]
            v_v[s * LEVELS + l] = v
            sums.append(v)
        decay = jnp.concatenate([decay_y[l], decay_y[l]], axis=1)
        both = jnp.where(forward_wide, decay * sums[0] + sums[1], sums[0] + decay * sums[1])
        col_out[2 * l] = both[:, 0:128]
        col_out[2 * l + 1] = both[:, 128:256]

    def row_states(l):
        for s in range(2):
            rows = slice(BLOCK * s, BLOCK * (s + 1))
            e1 = mm(sx_v[l], uh_v[l, rows, :], NT)
            e2 = mm(sx_v[l], ul_v[l, rows, :], NT)
            row_out[2 * l + s, :, 0:256] = e1[0:8] + e1[8:16] + e2[0:8]

    for group in GROUPS:
        for l in group:
            load(l).wait()
        for l in group:
            column_states(l)
        for l in group:
            row_states(l)

    v_h, v_l = halves(v_v[...].reshape(128, BLOCK))
    sxh = jnp.concatenate([sxh_v[...], sxh_v[...]], axis=0).astype(bf16)
    sxl = jnp.concatenate([sxl_v[...], sxl_v[...]], axis=0).astype(bf16)
    corner = mm(v_h, sxh, NT) + (mm(v_l, sxh, NT) + mm(v_h, sxl, NT))
    own = iota((128, 128), 0) // 8 == iota((128, 128), 1) // 8
    corner = jnp.sum(jnp.where(own, corner, 0.0).reshape(16, 8, 128), axis=0)

    @pl.loop(0, PEERS)
    def _(q):
        row_out[q, :, 256:384] = corner

    pl.semaphore_wait(barrier, 2 * (PEERS - 1))

    def row_copy(peer, there, src, dst, send, recv):
        return pltpu.make_async_remote_copy(
            src_ref=src.at[peer], dst_ref=dst.at[there], send_sem=send.at[peer], recv_sem=recv.at[there],
            device_id=(peer, c), device_id_type=MESH,
        )

    def col_copy(peer, there, src, dst, send, recv):
        rows = pl.ds(0, 8 if src is col_out else 12)
        return pltpu.make_async_remote_copy(
            src_ref=src.at[peer, rows], dst_ref=dst.at[there, rows], send_sem=send.at[peer], recv_sem=recv.at[there],
            device_id=(r, peer), device_id_type=MESH,
        )

    row1 = (row_out, row_in, row_send, row_recv)
    col1 = (col_out, col_in, col_send, col_recv)
    row2 = (row_out2, row_in2, row_send2, row_recv2)
    col2 = (col_out2, col_in2, col_send2, col_recv2)

    rows_to, cols_to = row_peers(r), col_peers(c)
    for row_peer, col_peer in zip(rows_to, cols_to):
        row_copy(row_peer, r, *row1).start()
        col_copy(col_peer, c, *col1).start()

    row_in[r] = row_out[r]
    col_in[c] = col_out[c]

    for l in range(LEVELS):

        def store_y(row, lane, high, low):
            ty_v[l, row : row + 16, lane : lane + 128] = high
            ty_v[l, row + 256 : row + 272, lane : lane + 128] = low

        def store_x(row, lane, high, low):
            txh_v[l, row : row + 16, lane : lane + 128] = high
            txl_v[l, row : row + 16, lane : lane + 128] = low

        toeplitz(*toeplitz_y[l], store_y)
        toeplitz(*toeplitz_x[l], store_x)

    for l in range(LEVELS):
        for s in range(2):
            rows = slice(BLOCK * s, BLOCK * (s + 1))
            d1 = mm(ty_v[l], uh_v[l, rows, :])
            d2 = mm(ty_v[l, 0:256, :], ul_v[l, rows, :])
            z_h, z_l = halves(d1[0:256] + d1[256:512] + d2)
            zh_v[l, rows, :] = z_h
            zl_v[l, rows, :] = z_l

    def local_field(l):
        p_out[l] = mm(zh_v[l], txh_v[l]) + (mm(zl_v[l], txh_v[l]) + mm(zh_v[l], txl_v[l]))

    for l in range(EARLY):
        local_field(l)

    sub, lane = iota(tile, 0), iota(tile, 1)
    level_of = (lane // 8) % LEVELS
    along_lanes = level_of * POLES + lane % POLES
    along_subs = level_of * POLES + sub % POLES

    def spread(ref, where_to):
        value = jnp.zeros(tile, f32)
        for n in range(LEVELS * POLES):
            value = jnp.where(where_to == n, ref[n % POLES, n // POLES], value)
        return value

    px_l, wx_l = spread(px, along_lanes), spread(wx, along_lanes)
    qx_l = 1.0 - px_l
    corner_decay_x = jnp.exp(log_of(qx_l) * BLOCK)
    square = (128, 128)
    stack = lambda t: jnp.concatenate([t] * 16, axis=0)
    p_c, q_c, g_c = stack(px_l), stack(qx_l), stack(wx_l * jnp.sqrt(1.0 - px_l * px_l))
    p_r, q_r, g_r = p_c.T, q_c.T, g_c.T
    row_id, lane_id = iota(square, 0), iota(square, 1)
    pair = (row_id // 8 == lane_id // 8) & (row_id % 8 < POLES) & (lane_id % 8 >= POLES)
    part = jnp.where(pair, g_r / (q_r + q_c - q_r * q_c), 0.0)
    total = jnp.sum(part, axis=0, keepdims=True)
    total = jnp.where(total > 0.0, total, 1.0)
    corner_mix_x = -(part * p_r) / total

    py_s, wy_s = spread(py, along_subs), spread(wy, along_subs)
    qy_s = 1.0 - py_s
    rate_y = log_of(qy_s)
    slab_decay_y, corner_decay_y = jnp.exp(rate_y * BLOCK), jnp.exp(rate_y * (2 * BLOCK))
    gy_s = wy_s * jnp.sqrt(1.0 - py_s * py_s)
    corner_mix_y, total = [], jnp.zeros(tile, f32)
    for k in range(POLES):
        row = lambda t: jnp.broadcast_to(t[k : k + 1, :], tile)
        q_k = row(qy_s)
        part = row(gy_s) / (qy_s + q_k - qy_s * q_k)
        total += part
        corner_mix_y.append(part * row(py_s))
    corner_mix_y = [-part / total for part in corner_mix_y]

    mix_x, rate_own = end_mix(px, wx, r // 2, (8, BLOCK))
    decay_own_x = jnp.exp(rate_own * BLOCK)
    mix_y, rate_own = end_mix(py, wy, c // 2, tile)
    decay_own_y = jnp.exp(rate_own * (2 * BLOCK))

    for peer in rows_to:
        row_copy(peer, peer, *row1).wait_recv()

    mine = jnp.full(tile, r, jnp.int32)
    corners = [row_in[i, :, 256:384] for i in range(PEERS)]
    state, enter_f = jnp.zeros(tile, f32), jnp.zeros(tile, f32)
    for i in range(PEERS):
        enter_f = jnp.where(mine == i, state, enter_f)
        state = corner_decay_x * state + corners[i]
    state = lax.dot_general(state, corner_mix_x, NN, precision=lax.Precision.HIGHEST, preferred_element_type=f32)
    enter_b = jnp.zeros(tile, f32)
    for i in range(PEERS - 1, -1, -1):
        enter_b = jnp.where(mine == i, state, enter_b)
        state = corner_decay_x * state + corners[i]
    corner = jnp.where(lane % 8 < POLES, enter_f, enter_b)
    swapped = pltpu.roll(corner, 64, 1)
    first = jnp.where(lane < 64, corner, swapped)
    second = jnp.where(lane < 64, swapped, corner)
    forward = sub < POLES
    both = jnp.where(forward, slab_decay_y * first + second, first + slab_decay_y * second)

    packed = jnp.where(lane < 64, both, pltpu.roll(both, POLES, 0))[0:POLES]

    for peer in cols_to:
        col_copy(peer, peer, *col1).wait_recv()

    entering = scan_blocks([col_in[i] for i in range(PEERS)], decay_own_y, mix_y)
    for i in range(PEERS):
        col_out2[i, 0:8, :] = entering[i]
        col_out2[i, 8:12, :] = packed

    for peer in cols_to:
        col_copy(peer, c, *col2).start()

    col_in2[c, 0:12, :] = col_out2[c, 0:12, :]

    entering = scan_blocks([row_in[i, :, 0:256] for i in range(PEERS)], decay_own_x, mix_x)
    f_h, f_l = halves(jnp.concatenate(entering, axis=0))
    high = mm(jnp.concatenate([f_h, f_l], axis=0), ty_v[r // 2, 0:256, :], NT)
    through = high[0:128] + (high[128:256] + mm(f_h, ty_v[r // 2, 256:512, :], NT))
    for i in range(PEERS):
        row_out2[i] = through[8 * i : 8 * i + 8]

    for peer in rows_to:
        row_copy(peer, r, *row2).start()

    row_in2[r] = row_out2[r]

    for row_peer, col_peer in zip(rows_to, cols_to):
        row_copy(row_peer, r, *row1).wait_send()
        col_copy(col_peer, c, *col1).wait_send()

    for l in range(EARLY, LEVELS):
        local_field(l)

    for row_peer, col_peer in zip(rows_to, cols_to):
        row_copy(row_peer, r, *row2).wait_send()
        col_copy(col_peer, c, *col2).wait_send()
    for peer in cols_to:
        col_copy(peer, peer, *col2).wait_recv()

    half = (POLES, 128)
    mine = jnp.full(half, c, jnp.int32)
    corners = [col_in2[i, 8:12, :] for i in range(PEERS)]
    decay = corner_decay_y[0:POLES]
    state, enter_f = jnp.zeros(half, f32), jnp.zeros(half, f32)
    for i in range(PEERS):
        enter_f = jnp.where(mine == i, state, enter_f)
        state = decay * state + corners[i]
    end = jnp.zeros(half, f32)
    for k in range(POLES):
        end += corner_mix_y[k][0:POLES] * jnp.broadcast_to(state[k : k + 1, :], half)
    turn = lambda t: pltpu.roll(jnp.concatenate([t, t], axis=0), 64, 1)
    state, enter_b = turn(end)[0:POLES], jnp.zeros(half, f32)
    for i in range(PEERS - 1, -1, -1):
        enter_b = jnp.where(mine == i, state, enter_b)
        state = decay * state + corners[i]
    twice = lambda t: jnp.concatenate([t, t], axis=0)
    enter_f = jnp.where(lane < 64, twice(enter_f), turn(enter_f))
    enter_b = jnp.where(lane < 64, turn(enter_b), twice(enter_b))
    corner_f = jnp.where(lane < 64, enter_f, slab_decay_y * enter_f + first)
    corner_b = jnp.where(lane < 64, slab_decay_y * enter_b + second, enter_b)
    corner = jnp.where(forward, corner_f, corner_b)

    spread_out = jnp.where(row_id // 8 == lane_id // 8, stack(corner), 0.0)
    k_h, k_l = halves(spread_out)
    ex_all = ex_v[...].reshape(64, BLOCK)
    x_h, x_l = halves(jnp.concatenate([ex_all, ex_all], axis=0))
    through = mm(k_h, x_h) + (mm(k_l, x_h) + mm(k_h, x_l))

    rounded = lambda t: t.astype(bf16).astype(f32)
    for l in range(LEVELS):
        decay = jnp.concatenate([decay_y[l], decay_y[l]], axis=1)
        enter = jnp.concatenate([col_in2[2 * l, 0:8, :], col_in2[2 * l + 1, 0:8, :]], axis=1)
        slabs = (
            jnp.where(forward_wide, enter, decay * enter + v_v[LEVELS + l]),
            jnp.where(forward_wide, decay * enter + v_v[l], enter),
        )
        e_h, e_l = halves(jnp.concatenate(slabs, axis=0))
        wide = mm(jnp.concatenate([e_h, e_l], axis=0), txh_v[l])
        wide = wide[0:16] + wide[16:32] + mm(e_h, txl_v[l])
        x_h = rounded(ex_v[l])
        x_l = ex_v[l] - x_h
        for s in range(2):
            at = 8 * (s * LEVELS + l)
            g = wide[8 * s : 8 * s + 8] + through[at : at + 8]
            g_h = rounded(g)
            g_l = g - g_h
            right_out[2 * l + s] = jnp.concatenate([x_h, x_h, x_l, g_h, g_l, g_h], axis=0).astype(bf16)

    for peer in rows_to:
        row_copy(peer, peer, *row2).wait_recv()

    for l in range(LEVELS):
        y_h = rounded(ey_v[l])
        y_l = ey_v[l] - y_h
        for s in range(2):
            f = row_in2[2 * l + s]
            f_h = rounded(f)
            f_l = f - f_h
            left_out[2 * l + s] = jnp.concatenate([f_h, f_l, f_h, y_h, y_h, y_l], axis=0).astype(bf16)


def kernel_field(p_ref, left_ref, right_ref, out_hbm, out_v, save_sem):
    save = lambda l: pltpu.make_async_copy(out_v.at[l], out_hbm.at[l], save_sem.at[l])

    for l in range(LEVELS):
        for s in range(2):
            rows = slice(BLOCK * s, BLOCK * (s + 1))
            out_v[l, rows, :] = jnp.exp(p_ref[l, rows, :] + mm(left_ref[2 * l + s], right_ref[2 * l + s], TN))
        save(l).start()

    @pl.loop(0, LEVELS)
    def _(l):
        save(l).wait()


def on_device(source, pole_x, weight_x, pole_y, weight_y):
    vmem = pl.BlockSpec(memory_space=pltpu.VMEM)
    hbm = pl.BlockSpec(memory_space=pltpu.HBM)
    shape = source.shape
    V = pltpu.VMEM
    sems = pltpu.SemaphoreType.DMA((PEERS,))
    local, left, right = pl.pallas_call(
        kernel_states,
        out_shape=(
            jax.ShapeDtypeStruct(shape, f32),
            jax.ShapeDtypeStruct((16, 48, BLOCK), bf16),
            jax.ShapeDtypeStruct((16, 48, BLOCK), bf16),
        ),
        in_specs=[hbm] * 5,
        out_specs=(vmem, vmem, vmem),
        scratch_shapes=[pltpu.SMEM((POLES, LEVELS), f32)] * 4 + [
            V(shape, f32), V(shape, bf16), V(shape, bf16), V(shape, bf16), V(shape, bf16),
            V((LEVELS, 512, BLOCK), bf16), V((LEVELS, 16, BLOCK), bf16), V((LEVELS, BLOCK, BLOCK), bf16), V((LEVELS, BLOCK, BLOCK), bf16),
            V((LEVELS, 16, BLOCK), bf16), V((64, BLOCK), f32), V((64, BLOCK), f32),
            V((LEVELS, 8, BLOCK), f32), V((LEVELS, 8, BLOCK), f32), V((LEVELS, 8, 128), f32),
            V((16, 8, BLOCK), f32),
            V((PEERS, 8, 384), f32), V((PEERS, 8, 384), f32), V((PEERS, 8, 128), f32), V((PEERS, 8, 128), f32),
            V((PEERS, 8, BLOCK), f32), V((PEERS, 8, BLOCK), f32), V((PEERS, 16, 128), f32), V((PEERS, 16, 128), f32),
            pltpu.SemaphoreType.DMA((4,)), pltpu.SemaphoreType.DMA((LEVELS,)),
        ] + [sems] * 8,
        compiler_params=pltpu.CompilerParams(collective_id=0, has_side_effects=True, vmem_limit_bytes=48 * 2**20),
    )(*(pltpu.with_memory_space_constraint(t.T, pltpu.HBM) for t in (pole_x, weight_x, pole_y, weight_y)), source)
    return pl.pallas_call(
        kernel_field,
        out_shape=jax.ShapeDtypeStruct(shape, f32),
        in_specs=[vmem] * 3,
        out_specs=hbm,
        scratch_shapes=[V(shape, f32), pltpu.SemaphoreType.DMA((LEVELS,))],
        compiler_params=pltpu.CompilerParams(vmem_limit_bytes=24 * 2**20),
    )(local, left, right)


def solution(mesh):
    return jax.shard_map(
        on_device,
        mesh=mesh,
        in_specs=(P(None, "col", "row"), P(), P(), P(), P()),
        out_specs=P(None, "col", "row"),
        check_vma=False,
    )
```

```python
import functools

import jax
import jax.numpy as jnp
from jax import lax
from jax.experimental import pallas as pl
from jax.experimental.pallas import tpu as pltpu
from jax.sharding import PartitionSpec as P

MESH = pl.DeviceIdType.MESH
LEVELS = 8
POLES = 4
BLOCK = 256
PEERS = 16
EARLY = 2
GROUPS = ((0, 1, 2), (3, 4, 5), (6, 7))
f32 = jnp.float32
bf16 = jnp.bfloat16
NN = (((1,), (0,)), ((), ()))
NT = (((1,), (1,)), ((), ()))
TN = (((0,), (0,)), ((), ()))


def mm(a, b, dims=NN):
    return lax.dot_general(a, b, dims, preferred_element_type=f32)


def halves(value):
    high = value.astype(bf16)
    return high, (value - high.astype(f32)).astype(bf16)


def iota(shape, dim):
    return lax.broadcasted_iota(jnp.int32, shape, dim)


def log_of(short):
    total = jnp.full_like(short, 1.0 / 7.0)
    for n in (6, 5, 4, 3, 2, 1):
        total = total * short + 1.0 / n
    return -short * total


def by_pole(ref, level, shape):
    place = iota(shape, 0) % POLES
    value = jnp.full(shape, ref[POLES - 1, level], f32)
    for k in range(POLES - 1):
        value = jnp.where(place == k, ref[k, level], value)
    return value


def couplings(short, decay, weight, shift):
    gain = jnp.sqrt(1.0 - decay * decay)
    forward, backward = weight * gain, weight * short
    sum_f = jnp.zeros_like(short)
    sum_b = jnp.zeros_like(short)
    for m in range(POLES):
        short_m, f_m, b_m = (short, forward, backward) if m == 0 else tuple(shift(t, m) for t in (short, forward, backward))
        share = 1.0 / (short + short_m - short * short_m)
        sum_f += b_m * share
        sum_b += f_m * share
    return forward, sum_b, forward * sum_f, backward * sum_b


def line_tables(pole_ref, weight_ref, level):
    shape = (8, 128)
    decay, weight = by_pole(pole_ref, level, shape), by_pole(weight_ref, level, shape)
    short = 1.0 - decay
    rate = log_of(short)
    _, _, c_f, c_b = couplings(short, decay, weight, lambda t, m: pltpu.roll(t, m, 0))
    forward = iota((8, BLOCK), 0) < POLES
    place = iota((8, BLOCK), 1)
    wide = lambda t: jnp.concatenate([t, t], axis=1)
    summary = jnp.exp(wide(rate) * jnp.where(forward, BLOCK - 1 - place, place).astype(f32))
    entry = jnp.exp(wide(rate) * jnp.where(forward, place + 1, BLOCK - place).astype(f32))
    entry = entry * jnp.where(forward, wide(c_f), wide(c_b))
    return rate, c_f, c_b, summary, entry


def toeplitz(rate, low, up, store):
    shape = (8, 128)
    sub, lane = iota(shape, 0), iota(shape, 1)
    apart = (sub - lane).astype(f32)
    rates = [jnp.broadcast_to(rate[k : k + 1, :], shape) for k in range(POLES)]
    step = [jnp.exp(8.0 * r) for r in rates]
    below = [jnp.broadcast_to(low[k : k + 1, :], shape) * jnp.exp(rates[k] * apart) for k in range(POLES)]
    above = [jnp.broadcast_to(up[k : k + 1, :], shape) * jnp.exp(rates[k] * (-120.0 - apart)) for k in range(POLES)]
    upper = {}
    for m in range(15, -17, -1):
        upper[m] = (above[0] + above[1]) + (above[2] + above[3])
        above = [a * s for a, s in zip(above, step)]
    tiles = {}
    for m in range(-16, 32):
        if m < 0:
            tiles[m] = upper[m]
            continue
        lower = (below[0] + below[1]) + (below[2] + below[3])
        below = [b * s for b, s in zip(below, step)]
        tiles[m] = lower if m > 15 else jnp.where(sub + 8 * m >= lane, lower, upper[m])
    for m in range(-16, 32, 2):
        high, low_part = halves(jnp.concatenate([tiles[m], tiles[m + 1]], axis=0))
        for j in range(2):
            if 0 <= m + 16 * j < 32:
                store(8 * (m + 16 * j), 128 * j, high, low_part)


def end_mix(pole_ref, weight_ref, level, shape):
    decay, weight = by_pole(pole_ref, level, shape), by_pole(weight_ref, level, shape)
    short = 1.0 - decay
    parts, total = [], jnp.zeros(shape, f32)
    for k in range(POLES):
        p_k = jnp.full(shape, pole_ref[k, level], f32)
        q_k = 1.0 - p_k
        part = weight_ref[k, level] * jnp.sqrt(1.0 - p_k * p_k) / (short + q_k - short * q_k)
        total += part
        parts.append(part * p_k)
    return [-part / total for part in parts], log_of(short)


def powers_of(decay):
    powers = [jnp.ones_like(decay)]
    for _ in range(PEERS - 1):
        powers.append(powers[-1] * decay)
    return powers[::-1]


def scan_blocks(inputs, decay, mix, powers):
    forward = iota(decay.shape, 0) < POLES
    ahead, back = jnp.zeros_like(decay), jnp.zeros_like(decay)
    before, behind = [], []
    for i in range(len(inputs)):
        before.append(ahead)
        behind.append(back)
        ahead = decay * ahead + inputs[i]
        back = decay * back + inputs[-1 - i]
    end = jnp.zeros_like(decay)
    for k in range(POLES):
        end += mix[k] * jnp.broadcast_to(ahead[k : k + 1, :], decay.shape)
    return [jnp.where(forward, f, b + w * end) for f, b, w in zip(before, behind[::-1], powers)]


def entry_weights(rate, span, here, forward):
    here = here.astype(f32)
    enter, end = [], []
    for i in range(PEERS):
        ahead, back = here - 1.0 - i, i - here - 1.0
        distance = jnp.where(forward, ahead, back)
        enter.append(jnp.where(distance >= 0.0, jnp.exp(rate * (span * jnp.maximum(distance, 0.0))), 0.0))
        end.append(jnp.exp(rate * (span * (PEERS - 1.0 - i))))
    return enter, end, jnp.where(forward, 0.0, jnp.exp(rate * (span * (PEERS - 1.0 - here))))


def weighted(blocks, weights):
    terms = [b * w for b, w in zip(blocks, weights)]
    while len(terms) > 1:
        terms = [terms[n] + terms[n + 1] for n in range(0, len(terms), 2)]
    return terms[0]


def row_peers(r):
    reach = (0, 1, 2, 1)
    steps = [(dx, dy) for dx in range(4) for dy in range(4) if dx or dy]
    steps.sort(key=lambda d: -(reach[d[0]] + reach[d[1]]))
    return [lax.rem(r // 4 + dx, 4) * 4 + lax.rem(lax.rem(r, 4) + dy, 4) for dx, dy in steps]


def col_peers(c):
    steps = [(dz, core) for dz in (4, 3, 5, 2, 6, 1, 7, 0) for core in (0, 1) if dz or core]
    return [lax.rem(c // 2 + dz, 8) * 2 + lax.rem(lax.rem(c, 2) + core, 2) for dz, core in steps]


def kernel_states(
    px_hbm, wx_hbm, py_hbm, wy_hbm, u_hbm, p_out, left_out, right_out,
    px, wx, py, wy, u_v, uh_v, ul_v, zh_v, zl_v, ty_v, sy_v, txh_v, txl_v, sx_v, sxh_v, sxl_v, ex_v, ey_v, decay_y, v_v,
    row_out, row_in, col_out, col_in, row_out2, row_in2, col_out2, col_in2,
    table_sem, load_sem, row_send, row_recv, col_send, col_recv, row_send2, row_recv2, col_send2, col_recv2,
):
    r, c = lax.axis_index("row"), lax.axis_index("col")
    load = lambda l: pltpu.make_async_copy(u_hbm.at[l], u_v.at[l], load_sem.at[l])

    tables = [
        pltpu.make_async_copy(src, dst, table_sem.at[n])
        for n, (src, dst) in enumerate(((px_hbm, px), (wx_hbm, wx), (py_hbm, py), (wy_hbm, wy)))
    ]
    for table in tables:
        table.start()

    @pl.loop(0, LEVELS)
    def _(l):
        load(l).start()

    barrier = pltpu.get_barrier_semaphore()

    @pl.loop(1, PEERS)
    def _(j):
        pl.semaphore_signal(barrier, inc=1, device_id=(lax.rem(r + j, PEERS), c), device_id_type=MESH)
        pl.semaphore_signal(barrier, inc=1, device_id=(r, lax.rem(c + j, PEERS)), device_id_type=MESH)

    tile = (8, 128)
    for table in tables:
        table.wait()

    toeplitz_x, toeplitz_y = [], []
    for l in range(LEVELS):
        rate, c_f, c_b, summary, entry = line_tables(px, wx, l)
        s_h, s_l = halves(summary)
        sx_v[l] = jnp.concatenate([s_h.astype(f32), s_l.astype(f32)], axis=0).astype(bf16)
        sxh_v[pl.ds(8 * l, 8), :] = s_h.astype(f32)
        sxl_v[pl.ds(8 * l, 8), :] = s_l.astype(f32)
        ex_v[l] = entry
        toeplitz_x.append((rate, c_b, c_f))

        rate, c_f, c_b, summary, entry = line_tables(py, wy, l)
        s_h, s_l = halves(summary)
        sy_v[l] = jnp.concatenate([s_h.astype(f32), s_l.astype(f32)], axis=0).astype(bf16)
        ey_v[l] = entry
        decay_y[l] = jnp.exp(rate * BLOCK)
        toeplitz_y.append((rate, c_f, c_b))

    forward_wide = iota((8, BLOCK), 0) < POLES

    def column_states(l):
        sums = []
        for s in range(2):
            rows = slice(BLOCK * s, BLOCK * (s + 1))
            u_h, u_l = halves(u_v[l, rows, :])
            uh_v[l, rows, :] = u_h
            ul_v[l, rows, :] = u_l
            d1 = mm(sy_v[l], u_h)
            d2 = mm(sy_v[l], u_l)
            v = d1[0:8] + d1[8:16] + d2[0:8]
            v_v[s * LEVELS + l] = v
            sums.append(v)
        decay = jnp.concatenate([decay_y[l], decay_y[l]], axis=1)
        both = jnp.where(forward_wide, decay * sums[0] + sums[1], sums[0] + decay * sums[1])
        col_out[2 * l] = both[:, 0:128]
        col_out[2 * l + 1] = both[:, 128:256]

    def row_states(l):
        for s in range(2):
            rows = slice(BLOCK * s, BLOCK * (s + 1))
            e1 = mm(sx_v[l], uh_v[l, rows, :], NT)
            e2 = mm(sx_v[l], ul_v[l, rows, :], NT)
            row_out[2 * l + s, :, 0:256] = e1[0:8] + e1[8:16] + e2[0:8]

    def corner_states():
        v_h, v_l = halves(v_v[...].reshape(128, BLOCK))
        sxh = jnp.concatenate([sxh_v[...], sxh_v[...]], axis=0).astype(bf16)
        sxl = jnp.concatenate([sxl_v[...], sxl_v[...]], axis=0).astype(bf16)
        corner = mm(v_h, sxh, NT) + (mm(v_l, sxh, NT) + mm(v_h, sxl, NT))
        own = iota((128, 128), 0) // 8 == iota((128, 128), 1) // 8
        corner = jnp.sum(jnp.where(own, corner, 0.0).reshape(16, 8, 128), axis=0)
        for q in range(PEERS):
            row_out[q, :, 256:384] = corner

    for group in GROUPS:
        for l in group:
            load(l).wait()
        for l in group:
            column_states(l)
        if group is GROUPS[-1]:
            corner_states()
        for l in group:
            row_states(l)

    pl.semaphore_wait(barrier, 2 * (PEERS - 1))

    def row_copy(peer, there, src, dst, send, recv):
        return pltpu.make_async_remote_copy(
            src_ref=src.at[peer], dst_ref=dst.at[there], send_sem=send.at[peer], recv_sem=recv.at[there],
            device_id=(peer, c), device_id_type=MESH,
        )

    def col_copy(peer, there, src, dst, send, recv):
        rows = pl.ds(0, 8 if src is col_out else 12)
        return pltpu.make_async_remote_copy(
            src_ref=src.at[peer, rows], dst_ref=dst.at[there, rows], send_sem=send.at[peer], recv_sem=recv.at[there],
            device_id=(r, peer), device_id_type=MESH,
        )

    row1 = (row_out, row_in, row_send, row_recv)
    col1 = (col_out, col_in, col_send, col_recv)
    row2 = (row_out2, row_in2, row_send2, row_recv2)
    col2 = (col_out2, col_in2, col_send2, col_recv2)

    rows_to, cols_to = row_peers(r), col_peers(c)
    for row_peer, col_peer in zip(rows_to, cols_to):
        row_copy(row_peer, r, *row1).start()
        col_copy(col_peer, c, *col1).start()

    row_in[r] = row_out[r]
    col_in[c] = col_out[c]

    for l in range(LEVELS):

        def store_y(row, lane, high, low):
            ty_v[l, row : row + 16, lane : lane + 128] = high
            ty_v[l, row + 256 : row + 272, lane : lane + 128] = low

        def store_x(row, lane, high, low):
            txh_v[l, row : row + 16, lane : lane + 128] = high
            txl_v[l, row : row + 16, lane : lane + 128] = low

        toeplitz(*toeplitz_y[l], store_y)
        toeplitz(*toeplitz_x[l], store_x)

    for l in range(LEVELS):
        for s in range(2):
            rows = slice(BLOCK * s, BLOCK * (s + 1))
            d1 = mm(ty_v[l], uh_v[l, rows, :])
            d2 = mm(ty_v[l, 0:256, :], ul_v[l, rows, :])
            z_h, z_l = halves(d1[0:256] + d1[256:512] + d2)
            zh_v[l, rows, :] = z_h
            zl_v[l, rows, :] = z_l

    def local_field(l):
        p_out[l] = mm(zh_v[l], txh_v[l]) + (mm(zl_v[l], txh_v[l]) + mm(zh_v[l], txl_v[l]))

    for l in range(EARLY):
        local_field(l)

    sub, lane = iota(tile, 0), iota(tile, 1)
    level_of = (lane // 8) % LEVELS
    along_lanes = level_of * POLES + lane % POLES
    along_subs = level_of * POLES + sub % POLES

    def spread(ref, where_to):
        value = jnp.zeros(tile, f32)
        for n in range(LEVELS * POLES):
            value = jnp.where(where_to == n, ref[n % POLES, n // POLES], value)
        return value

    px_l, wx_l = spread(px, along_lanes), spread(wx, along_lanes)
    qx_l = 1.0 - px_l
    enter_x, end_x, back_x = entry_weights(log_of(qx_l), float(BLOCK), jnp.full(tile, r, jnp.int32), lane % 8 < POLES)
    square = (128, 128)
    stack = lambda t: jnp.concatenate([t] * 16, axis=0)
    p_c, q_c, g_c = stack(px_l), stack(qx_l), stack(wx_l * jnp.sqrt(1.0 - px_l * px_l))
    p_r, q_r, g_r = p_c.T, q_c.T, g_c.T
    row_id, lane_id = iota(square, 0), iota(square, 1)
    pair = (row_id // 8 == lane_id // 8) & (row_id % 8 < POLES) & (lane_id % 8 >= POLES)
    part = jnp.where(pair, g_r / (q_r + q_c - q_r * q_c), 0.0)
    total = jnp.sum(part, axis=0, keepdims=True)
    total = jnp.where(total > 0.0, total, 1.0)
    corner_mix_x = -(part * p_r) / total
    roll_mix_x = [
        jnp.broadcast_to(jnp.sum(jnp.where(row_id == lane_id - d, corner_mix_x, 0.0), axis=0, keepdims=True), tile)
        for d in range(1, 8)
    ]

    py_s, wy_s = spread(py, along_subs), spread(wy, along_subs)
    qy_s = 1.0 - py_s
    rate_y = log_of(qy_s)
    slab_decay_y = jnp.exp(rate_y * BLOCK)
    half = (POLES, 128)
    enter_y, end_y, back_y = entry_weights(
        rate_y[0:POLES], 2.0 * BLOCK, jnp.full(half, c, jnp.int32), iota(half, 1) < 64
    )
    gy_s = wy_s * jnp.sqrt(1.0 - py_s * py_s)
    corner_mix_y, total = [], jnp.zeros(tile, f32)
    for k in range(POLES):
        row = lambda t: jnp.broadcast_to(t[k : k + 1, :], tile)
        q_k = row(qy_s)
        part = row(gy_s) / (qy_s + q_k - qy_s * q_k)
        total += part
        corner_mix_y.append(part * row(py_s))
    corner_mix_y = [-part / total for part in corner_mix_y]

    mix_x, rate_own = end_mix(px, wx, r // 2, (8, BLOCK))
    decay_own_x = jnp.exp(rate_own * BLOCK)
    mix_y, rate_own = end_mix(py, wy, c // 2, tile)
    decay_own_y = jnp.exp(rate_own * (2 * BLOCK))
    powers_x, powers_y = powers_of(decay_own_x), powers_of(decay_own_y)

    for peer in rows_to:
        row_copy(peer, peer, *row1).wait_recv()

    corners = [row_in[i, :, 256:384] for i in range(PEERS)]
    end = weighted(corners, end_x)
    end = weighted([pltpu.roll(end, d, 1) for d in range(1, 8)] + [jnp.zeros(tile, f32)], roll_mix_x + [end])
    corner = weighted(corners, enter_x) + back_x * end
    swapped = pltpu.roll(corner, 64, 1)
    first = jnp.where(lane < 64, corner, swapped)
    second = jnp.where(lane < 64, swapped, corner)
    forward = sub < POLES
    both = jnp.where(forward, slab_decay_y * first + second, first + slab_decay_y * second)

    packed = jnp.where(lane < 64, both, pltpu.roll(both, POLES, 0))[0:POLES]

    for peer in cols_to:
        col_copy(peer, peer, *col1).wait_recv()

    entering = scan_blocks([col_in[i] for i in range(PEERS)], decay_own_y, mix_y, powers_y)
    for i in range(PEERS):
        col_out2[i, 0:8, :] = entering[i]
        col_out2[i, 8:12, :] = packed

    for peer in cols_to:
        col_copy(peer, c, *col2).start()

    col_in2[c, 0:12, :] = col_out2[c, 0:12, :]

    entering = scan_blocks([row_in[i, :, 0:256] for i in range(PEERS)], decay_own_x, mix_x, powers_x)
    f_h, f_l = halves(jnp.concatenate(entering, axis=0))
    high = mm(jnp.concatenate([f_h, f_l], axis=0), ty_v[r // 2, 0:256, :], NT)
    through = high[0:128] + (high[128:256] + mm(f_h, ty_v[r // 2, 256:512, :], NT))
    for i in range(PEERS):
        row_out2[i] = through[8 * i : 8 * i + 8]

    for peer in rows_to:
        row_copy(peer, r, *row2).start()

    row_in2[r] = row_out2[r]

    for row_peer, col_peer in zip(rows_to, cols_to):
        row_copy(row_peer, r, *row1).wait_send()
        col_copy(col_peer, c, *col1).wait_send()

    for l in range(EARLY, LEVELS):
        local_field(l)

    for row_peer, col_peer in zip(rows_to, cols_to):
        row_copy(row_peer, r, *row2).wait_send()
        col_copy(col_peer, c, *col2).wait_send()
    for peer in cols_to:
        col_copy(peer, peer, *col2).wait_recv()

    corners = [col_in2[i, 8:12, :] for i in range(PEERS)]
    state = weighted(corners, end_y)
    end = jnp.zeros(half, f32)
    for k in range(POLES):
        end += corner_mix_y[k][0:POLES] * jnp.broadcast_to(state[k : k + 1, :], half)
    turn = lambda t: pltpu.roll(jnp.concatenate([t, t], axis=0), 64, 1)
    enter = weighted(corners, enter_y) + back_y * turn(end)[0:POLES]
    twice = lambda t: jnp.concatenate([t, t], axis=0)
    enter_f = jnp.where(lane < 64, twice(enter), turn(enter))
    enter_b = jnp.where(lane < 64, turn(enter), twice(enter))
    corner_f = jnp.where(lane < 64, enter_f, slab_decay_y * enter_f + first)
    corner_b = jnp.where(lane < 64, slab_decay_y * enter_b + second, enter_b)
    corner = jnp.where(forward, corner_f, corner_b)

    spread_out = jnp.where(row_id // 8 == lane_id // 8, stack(corner), 0.0)
    k_h, k_l = halves(spread_out)
    ex_all = ex_v[...].reshape(64, BLOCK)
    x_h, x_l = halves(jnp.concatenate([ex_all, ex_all], axis=0))
    through = mm(k_h, x_h) + (mm(k_l, x_h) + mm(k_h, x_l))

    rounded = lambda t: t.astype(bf16).astype(f32)
    for l in range(LEVELS):
        decay = jnp.concatenate([decay_y[l], decay_y[l]], axis=1)
        enter = jnp.concatenate([col_in2[2 * l, 0:8, :], col_in2[2 * l + 1, 0:8, :]], axis=1)
        slabs = (
            jnp.where(forward_wide, enter, decay * enter + v_v[LEVELS + l]),
            jnp.where(forward_wide, decay * enter + v_v[l], enter),
        )
        e_h, e_l = halves(jnp.concatenate(slabs, axis=0))
        wide = mm(jnp.concatenate([e_h, e_l], axis=0), txh_v[l])
        wide = wide[0:16] + wide[16:32] + mm(e_h, txl_v[l])
        x_h = rounded(ex_v[l])
        x_l = ex_v[l] - x_h
        for s in range(2):
            at = 8 * (s * LEVELS + l)
            g = wide[8 * s : 8 * s + 8] + through[at : at + 8]
            g_h = rounded(g)
            g_l = g - g_h
            right_out[2 * l + s] = jnp.concatenate([x_h, x_h, x_l, g_h, g_l, g_h], axis=0).astype(bf16)

    for peer in rows_to:
        row_copy(peer, peer, *row2).wait_recv()

    for l in range(LEVELS):
        y_h = rounded(ey_v[l])
        y_l = ey_v[l] - y_h
        for s in range(2):
            f = row_in2[2 * l + s]
            f_h = rounded(f)
            f_l = f - f_h
            left_out[2 * l + s] = jnp.concatenate([f_h, f_l, f_h, y_h, y_h, y_l], axis=0).astype(bf16)


def kernel_field(p_ref, left_ref, right_ref, out_hbm, out_v, save_sem):
    save = lambda l: pltpu.make_async_copy(out_v.at[l], out_hbm.at[l], save_sem.at[l])

    for l in range(LEVELS):
        for s in range(2):
            rows = slice(BLOCK * s, BLOCK * (s + 1))
            out_v[l, rows, :] = jnp.exp(p_ref[l, rows, :] + mm(left_ref[2 * l + s], right_ref[2 * l + s], TN))
        save(l).start()

    @pl.loop(0, LEVELS)
    def _(l):
        save(l).wait()


def on_device(source, pole_x, weight_x, pole_y, weight_y):
    vmem = pl.BlockSpec(memory_space=pltpu.VMEM)
    hbm = pl.BlockSpec(memory_space=pltpu.HBM)
    shape = source.shape
    V = pltpu.VMEM
    sems = pltpu.SemaphoreType.DMA((PEERS,))
    local, left, right = pl.pallas_call(
        kernel_states,
        out_shape=(
            jax.ShapeDtypeStruct(shape, f32),
            jax.ShapeDtypeStruct((16, 48, BLOCK), bf16),
            jax.ShapeDtypeStruct((16, 48, BLOCK), bf16),
        ),
        in_specs=[hbm] * 5,
        out_specs=(vmem, vmem, vmem),
        scratch_shapes=[pltpu.SMEM((POLES, LEVELS), f32)] * 4 + [
            V(shape, f32), V(shape, bf16), V(shape, bf16), V(shape, bf16), V(shape, bf16),
            V((LEVELS, 512, BLOCK), bf16), V((LEVELS, 16, BLOCK), bf16), V((LEVELS, BLOCK, BLOCK), bf16), V((LEVELS, BLOCK, BLOCK), bf16),
            V((LEVELS, 16, BLOCK), bf16), V((64, BLOCK), f32), V((64, BLOCK), f32),
            V((LEVELS, 8, BLOCK), f32), V((LEVELS, 8, BLOCK), f32), V((LEVELS, 8, 128), f32),
            V((16, 8, BLOCK), f32),
            V((PEERS, 8, 384), f32), V((PEERS, 8, 384), f32), V((PEERS, 8, 128), f32), V((PEERS, 8, 128), f32),
            V((PEERS, 8, BLOCK), f32), V((PEERS, 8, BLOCK), f32), V((PEERS, 16, 128), f32), V((PEERS, 16, 128), f32),
            pltpu.SemaphoreType.DMA((4,)), pltpu.SemaphoreType.DMA((LEVELS,)),
        ] + [sems] * 8,
        compiler_params=pltpu.CompilerParams(collective_id=0, has_side_effects=True, vmem_limit_bytes=48 * 2**20),
    )(*(pltpu.with_memory_space_constraint(t.T, pltpu.HBM) for t in (pole_x, weight_x, pole_y, weight_y)), source)
    return pl.pallas_call(
        kernel_field,
        out_shape=jax.ShapeDtypeStruct(shape, f32),
        in_specs=[vmem] * 3,
        out_specs=hbm,
        scratch_shapes=[V(shape, f32), pltpu.SemaphoreType.DMA((LEVELS,))],
        compiler_params=pltpu.CompilerParams(vmem_limit_bytes=24 * 2**20),
    )(local, left, right)


def solution(mesh):
    return jax.shard_map(
        on_device,
        mesh=mesh,
        in_specs=(P(None, "col", "row"), P(), P(), P(), P()),
        out_specs=P(None, "col", "row"),
        check_vma=False,
    )
```

```python
import functools

import jax
import jax.numpy as jnp
from jax import lax
from jax.experimental import pallas as pl
from jax.experimental.pallas import tpu as pltpu
from jax.sharding import PartitionSpec as P

MESH = pl.DeviceIdType.MESH
LEVELS = 8
POLES = 4
BLOCK = 256
PEERS = 16
EARLY = 2
GROUPS = ((0, 1), (2, 3, 4), (5, 6, 7))
f32 = jnp.float32
bf16 = jnp.bfloat16
NN = (((1,), (0,)), ((), ()))
NT = (((1,), (1,)), ((), ()))
TN = (((0,), (0,)), ((), ()))


def mm(a, b, dims=NN):
    return lax.dot_general(a, b, dims, preferred_element_type=f32)


def halves(value):
    high = value.astype(bf16)
    return high, (value - high.astype(f32)).astype(bf16)


def iota(shape, dim):
    return lax.broadcasted_iota(jnp.int32, shape, dim)


def log_of(short):
    total = jnp.full_like(short, 1.0 / 7.0)
    for n in (6, 5, 4, 3, 2, 1):
        total = total * short + 1.0 / n
    return -short * total


def by_pole(ref, level, shape):
    place = iota(shape, 0) % POLES
    value = jnp.full(shape, ref[POLES - 1, level], f32)
    for k in range(POLES - 1):
        value = jnp.where(place == k, ref[k, level], value)
    return value


def couplings(short, decay, weight, shift):
    gain = jnp.sqrt(1.0 - decay * decay)
    forward, backward = weight * gain, weight * short
    sum_f = jnp.zeros_like(short)
    sum_b = jnp.zeros_like(short)
    for m in range(POLES):
        short_m, f_m, b_m = (short, forward, backward) if m == 0 else tuple(shift(t, m) for t in (short, forward, backward))
        share = 1.0 / (short + short_m - short * short_m)
        sum_f += b_m * share
        sum_b += f_m * share
    return forward, sum_b, forward * sum_f, backward * sum_b


def line_tables(pole_ref, weight_ref, level):
    shape = (8, 128)
    decay, weight = by_pole(pole_ref, level, shape), by_pole(weight_ref, level, shape)
    short = 1.0 - decay
    rate = log_of(short)
    _, _, c_f, c_b = couplings(short, decay, weight, lambda t, m: pltpu.roll(t, m, 0))
    forward = iota((8, BLOCK), 0) < POLES
    place = iota((8, BLOCK), 1)
    wide = lambda t: jnp.concatenate([t, t], axis=1)
    summary = jnp.exp(wide(rate) * jnp.where(forward, BLOCK - 1 - place, place).astype(f32))
    entry = jnp.exp(wide(rate) * jnp.where(forward, place + 1, BLOCK - place).astype(f32))
    entry = entry * jnp.where(forward, wide(c_f), wide(c_b))
    return rate, c_f, c_b, summary, entry


def toeplitz(rate, low, up, store):
    shape = (8, 128)
    sub, lane = iota(shape, 0), iota(shape, 1)
    apart = (sub - lane).astype(f32)
    rates = [jnp.broadcast_to(rate[k : k + 1, :], shape) for k in range(POLES)]
    step = [jnp.exp(8.0 * r) for r in rates]
    below = [jnp.broadcast_to(low[k : k + 1, :], shape) * jnp.exp(rates[k] * apart) for k in range(POLES)]
    above = [jnp.broadcast_to(up[k : k + 1, :], shape) * jnp.exp(rates[k] * (-120.0 - apart)) for k in range(POLES)]
    upper = {}
    for m in range(15, -17, -1):
        upper[m] = (above[0] + above[1]) + (above[2] + above[3])
        above = [a * s for a, s in zip(above, step)]
    tiles = {}
    for m in range(-16, 32):
        if m < 0:
            tiles[m] = upper[m]
            continue
        lower = (below[0] + below[1]) + (below[2] + below[3])
        below = [b * s for b, s in zip(below, step)]
        tiles[m] = lower if m > 15 else jnp.where(sub + 8 * m >= lane, lower, upper[m])
    for m in range(-16, 32, 2):
        high, low_part = halves(jnp.concatenate([tiles[m], tiles[m + 1]], axis=0))
        for j in range(2):
            if 0 <= m + 16 * j < 32:
                store(8 * (m + 16 * j), 128 * j, high, low_part)


def end_mix(pole_ref, weight_ref, level, shape):
    decay, weight = by_pole(pole_ref, level, shape), by_pole(weight_ref, level, shape)
    short = 1.0 - decay
    parts, total = [], jnp.zeros(shape, f32)
    for k in range(POLES):
        p_k = jnp.full(shape, pole_ref[k, level], f32)
        q_k = 1.0 - p_k
        part = weight_ref[k, level] * jnp.sqrt(1.0 - p_k * p_k) / (short + q_k - short * q_k)
        total += part
        parts.append(part * p_k)
    return [-part / total for part in parts], log_of(short)


def powers_of(decay):
    powers = [jnp.ones_like(decay)]
    for _ in range(PEERS - 1):
        powers.append(powers[-1] * decay)
    return powers[::-1]


def scan_blocks(inputs, decay, mix, powers):
    forward = iota(decay.shape, 0) < POLES
    ahead, back = jnp.zeros_like(decay), jnp.zeros_like(decay)
    before, behind = [], []
    for i in range(len(inputs)):
        before.append(ahead)
        behind.append(back)
        ahead = decay * ahead + inputs[i]
        back = decay * back + inputs[-1 - i]
    end = jnp.zeros_like(decay)
    for k in range(POLES):
        end += mix[k] * jnp.broadcast_to(ahead[k : k + 1, :], decay.shape)
    return [jnp.where(forward, f, b + w * end) for f, b, w in zip(before, behind[::-1], powers)]


def entry_weights(rate, span, here, forward):
    here = here.astype(f32)
    enter, end = [], []
    for i in range(PEERS):
        ahead, back = here - 1.0 - i, i - here - 1.0
        distance = jnp.where(forward, ahead, back)
        enter.append(jnp.where(distance >= 0.0, jnp.exp(rate * (span * jnp.maximum(distance, 0.0))), 0.0))
        end.append(jnp.exp(rate * (span * (PEERS - 1.0 - i))))
    return enter, end, jnp.where(forward, 0.0, jnp.exp(rate * (span * (PEERS - 1.0 - here))))


def weighted(blocks, weights):
    terms = [b * w for b, w in zip(blocks, weights)]
    while len(terms) > 1:
        terms = [terms[n] + terms[n + 1] for n in range(0, len(terms), 2)]
    return terms[0]


def row_peers(r):
    reach = (0, 1, 2, 1)
    steps = [(dx, dy) for dx in range(4) for dy in range(4) if dx or dy]
    steps.sort(key=lambda d: -(reach[d[0]] + reach[d[1]]))
    return [lax.rem(r // 4 + dx, 4) * 4 + lax.rem(lax.rem(r, 4) + dy, 4) for dx, dy in steps]


def col_peers(c):
    steps = [(dz, core) for dz in (4, 3, 5, 2, 6, 1, 7, 0) for core in (0, 1) if dz or core]
    return [lax.rem(c // 2 + dz, 8) * 2 + lax.rem(lax.rem(c, 2) + core, 2) for dz, core in steps]


def kernel_states(
    px_hbm, wx_hbm, py_hbm, wy_hbm, u_hbm, p_out, left_out, right_out,
    px, wx, py, wy, u_v, uh_v, ul_v, zh_v, zl_v, ty_v, sy_v, txh_v, txl_v, sx_v, sxh_v, sxl_v, ex_v, ey_v, decay_y, v_v,
    row_out, row_in, corner_out, corner_in, col_out, col_in, row_out2, row_in2, col_out2, col_in2,
    table_sem, load_sem, row_send, row_recv, corner_send, corner_recv, col_send, col_recv, row_send2, row_recv2, col_send2, col_recv2,
):
    r, c = lax.axis_index("row"), lax.axis_index("col")
    load = lambda l: pltpu.make_async_copy(u_hbm.at[l], u_v.at[l], load_sem.at[l])

    tables = [
        pltpu.make_async_copy(src, dst, table_sem.at[n])
        for n, (src, dst) in enumerate(((px_hbm, px), (wx_hbm, wx), (py_hbm, py), (wy_hbm, wy)))
    ]
    for table in tables:
        table.start()

    @pl.loop(0, LEVELS)
    def _(l):
        load(l).start()

    barrier = pltpu.get_barrier_semaphore()

    @pl.loop(1, PEERS)
    def _(j):
        pl.semaphore_signal(barrier, inc=1, device_id=(lax.rem(r + j, PEERS), c), device_id_type=MESH)
        pl.semaphore_signal(barrier, inc=1, device_id=(r, lax.rem(c + j, PEERS)), device_id_type=MESH)

    tile = (8, 128)
    for table in tables:
        table.wait()

    toeplitz_x, toeplitz_y = [], []
    for l in range(LEVELS):
        rate, c_f, c_b, summary, entry = line_tables(px, wx, l)
        s_h, s_l = halves(summary)
        sx_v[l] = jnp.concatenate([s_h.astype(f32), s_l.astype(f32)], axis=0).astype(bf16)
        sxh_v[pl.ds(8 * l, 8), :] = s_h.astype(f32)
        sxl_v[pl.ds(8 * l, 8), :] = s_l.astype(f32)
        ex_v[l] = entry
        toeplitz_x.append((rate, c_b, c_f))

        rate, c_f, c_b, summary, entry = line_tables(py, wy, l)
        s_h, s_l = halves(summary)
        sy_v[l] = jnp.concatenate([s_h.astype(f32), s_l.astype(f32)], axis=0).astype(bf16)
        ey_v[l] = entry
        decay_y[l] = jnp.exp(rate * BLOCK)
        toeplitz_y.append((rate, c_f, c_b))

    forward_wide = iota((8, BLOCK), 0) < POLES

    def column_states(l):
        sums = []
        for s in range(2):
            rows = slice(BLOCK * s, BLOCK * (s + 1))
            u_h, u_l = halves(u_v[l, rows, :])
            uh_v[l, rows, :] = u_h
            ul_v[l, rows, :] = u_l
            d1 = mm(sy_v[l], u_h)
            d2 = mm(sy_v[l], u_l)
            v = d1[0:8] + d1[8:16] + d2[0:8]
            v_v[s * LEVELS + l] = v
            sums.append(v)
        decay = jnp.concatenate([decay_y[l], decay_y[l]], axis=1)
        both = jnp.where(forward_wide, decay * sums[0] + sums[1], sums[0] + decay * sums[1])
        col_out[2 * l] = both[:, 0:128]
        col_out[2 * l + 1] = both[:, 128:256]

    def row_states(l):
        for s in range(2):
            rows = slice(BLOCK * s, BLOCK * (s + 1))
            e1 = mm(sx_v[l], uh_v[l, rows, :], NT)
            e2 = mm(sx_v[l], ul_v[l, rows, :], NT)
            row_out[2 * l + s] = e1[0:8] + e1[8:16] + e2[0:8]

    def corner_states():
        v_h, v_l = halves(v_v[...].reshape(128, BLOCK))
        sxh = jnp.concatenate([sxh_v[...], sxh_v[...]], axis=0).astype(bf16)
        sxl = jnp.concatenate([sxl_v[...], sxl_v[...]], axis=0).astype(bf16)
        corner = mm(v_h, sxh, NT) + (mm(v_l, sxh, NT) + mm(v_h, sxl, NT))
        own = iota((128, 128), 0) // 8 == iota((128, 128), 1) // 8
        corner = jnp.sum(jnp.where(own, corner, 0.0).reshape(16, 8, 128), axis=0)
        corner_out[0] = corner

    for n, group in enumerate(GROUPS):
        for l in group:
            load(l).wait()
        for l in group:
            column_states(l)
        if n >= 1:
            for l in GROUPS[n - 1]:
                row_states(l)
    corner_states()

    pl.semaphore_wait(barrier, 2 * (PEERS - 1))

    def row_copy(peer, there, src, dst, send, recv):
        return pltpu.make_async_remote_copy(
            src_ref=src.at[peer], dst_ref=dst.at[there], send_sem=send.at[peer], recv_sem=recv.at[there],
            device_id=(peer, c), device_id_type=MESH,
        )

    def col_copy(peer, there, src, dst, send, recv):
        rows = pl.ds(0, 8 if src is col_out else 12)
        return pltpu.make_async_remote_copy(
            src_ref=src.at[peer, rows], dst_ref=dst.at[there, rows], send_sem=send.at[peer], recv_sem=recv.at[there],
            device_id=(r, peer), device_id_type=MESH,
        )

    def corner_copy(peer, there):
        return pltpu.make_async_remote_copy(
            src_ref=corner_out.at[0], dst_ref=corner_in.at[there], send_sem=corner_send.at[peer],
            recv_sem=corner_recv.at[there], device_id=(peer, c), device_id_type=MESH,
        )

    row1 = (row_out, row_in, row_send, row_recv)
    col1 = (col_out, col_in, col_send, col_recv)
    row2 = (row_out2, row_in2, row_send2, row_recv2)
    col2 = (col_out2, col_in2, col_send2, col_recv2)

    rows_to, cols_to = row_peers(r), col_peers(c)
    for row_peer, col_peer in zip(rows_to, cols_to):
        corner_copy(row_peer, r).start()
        col_copy(col_peer, c, *col1).start()

    for l in GROUPS[-1]:
        row_states(l)

    for peer in rows_to:
        row_copy(peer, r, *row1).start()

    corner_in[r] = corner_out[0]
    row_in[r] = row_out[r]
    col_in[c] = col_out[c]

    for l in range(LEVELS):

        def store_y(row, lane, high, low):
            ty_v[l, row : row + 16, lane : lane + 128] = high
            ty_v[l, row + 256 : row + 272, lane : lane + 128] = low

        def store_x(row, lane, high, low):
            txh_v[l, row : row + 16, lane : lane + 128] = high
            txl_v[l, row : row + 16, lane : lane + 128] = low

        toeplitz(*toeplitz_y[l], store_y)
        toeplitz(*toeplitz_x[l], store_x)

    for l in range(LEVELS):
        for s in range(2):
            rows = slice(BLOCK * s, BLOCK * (s + 1))
            d1 = mm(ty_v[l], uh_v[l, rows, :])
            d2 = mm(ty_v[l, 0:256, :], ul_v[l, rows, :])
            z_h, z_l = halves(d1[0:256] + d1[256:512] + d2)
            zh_v[l, rows, :] = z_h
            zl_v[l, rows, :] = z_l

    def local_field(l):
        p_out[l] = mm(zh_v[l], txh_v[l]) + (mm(zl_v[l], txh_v[l]) + mm(zh_v[l], txl_v[l]))

    for l in range(EARLY):
        local_field(l)

    sub, lane = iota(tile, 0), iota(tile, 1)
    level_of = (lane // 8) % LEVELS
    along_lanes = level_of * POLES + lane % POLES
    along_subs = level_of * POLES + sub % POLES

    def spread(ref, where_to):
        value = jnp.zeros(tile, f32)
        for n in range(LEVELS * POLES):
            value = jnp.where(where_to == n, ref[n % POLES, n // POLES], value)
        return value

    px_l, wx_l = spread(px, along_lanes), spread(wx, along_lanes)
    qx_l = 1.0 - px_l
    enter_x, end_x, back_x = entry_weights(log_of(qx_l), float(BLOCK), jnp.full(tile, r, jnp.int32), lane % 8 < POLES)
    square = (128, 128)
    stack = lambda t: jnp.concatenate([t] * 16, axis=0)
    p_c, q_c, g_c = stack(px_l), stack(qx_l), stack(wx_l * jnp.sqrt(1.0 - px_l * px_l))
    p_r, q_r, g_r = p_c.T, q_c.T, g_c.T
    row_id, lane_id = iota(square, 0), iota(square, 1)
    pair = (row_id // 8 == lane_id // 8) & (row_id % 8 < POLES) & (lane_id % 8 >= POLES)
    part = jnp.where(pair, g_r / (q_r + q_c - q_r * q_c), 0.0)
    total = jnp.sum(part, axis=0, keepdims=True)
    total = jnp.where(total > 0.0, total, 1.0)
    corner_mix_x = -(part * p_r) / total
    roll_mix_x = [
        jnp.broadcast_to(jnp.sum(jnp.where(row_id == lane_id - d, corner_mix_x, 0.0), axis=0, keepdims=True), tile)
        for d in range(1, 8)
    ]

    py_s, wy_s = spread(py, along_subs), spread(wy, along_subs)
    qy_s = 1.0 - py_s
    rate_y = log_of(qy_s)
    slab_decay_y = jnp.exp(rate_y * BLOCK)
    half = (POLES, 128)
    enter_y, end_y, back_y = entry_weights(
        rate_y[0:POLES], 2.0 * BLOCK, jnp.full(half, c, jnp.int32), iota(half, 1) < 64
    )
    gy_s = wy_s * jnp.sqrt(1.0 - py_s * py_s)
    corner_mix_y, total = [], jnp.zeros(tile, f32)
    for k in range(POLES):
        row = lambda t: jnp.broadcast_to(t[k : k + 1, :], tile)
        q_k = row(qy_s)
        part = row(gy_s) / (qy_s + q_k - qy_s * q_k)
        total += part
        corner_mix_y.append(part * row(py_s))
    corner_mix_y = [-part / total for part in corner_mix_y]

    mix_x, rate_own = end_mix(px, wx, r // 2, (8, BLOCK))
    decay_own_x = jnp.exp(rate_own * BLOCK)
    mix_y, rate_own = end_mix(py, wy, c // 2, tile)
    decay_own_y = jnp.exp(rate_own * (2 * BLOCK))
    powers_x, powers_y = powers_of(decay_own_x), powers_of(decay_own_y)

    for peer in rows_to:
        corner_copy(peer, peer).wait_recv()

    corners = [corner_in[i] for i in range(PEERS)]
    end = weighted(corners, end_x)
    end = weighted([pltpu.roll(end, d, 1) for d in range(1, 8)] + [jnp.zeros(tile, f32)], roll_mix_x + [end])
    corner = weighted(corners, enter_x) + back_x * end
    swapped = pltpu.roll(corner, 64, 1)
    first = jnp.where(lane < 64, corner, swapped)
    second = jnp.where(lane < 64, swapped, corner)
    forward = sub < POLES
    both = jnp.where(forward, slab_decay_y * first + second, first + slab_decay_y * second)

    packed = jnp.where(lane < 64, both, pltpu.roll(both, POLES, 0))[0:POLES]

    for peer in cols_to:
        col_copy(peer, peer, *col1).wait_recv()

    entering = scan_blocks([col_in[i] for i in range(PEERS)], decay_own_y, mix_y, powers_y)
    for i in range(PEERS):
        col_out2[i, 0:8, :] = entering[i]
        col_out2[i, 8:12, :] = packed

    for peer in cols_to:
        col_copy(peer, c, *col2).start()

    col_in2[c, 0:12, :] = col_out2[c, 0:12, :]

    for peer in rows_to:
        row_copy(peer, peer, *row1).wait_recv()

    entering = scan_blocks([row_in[i] for i in range(PEERS)], decay_own_x, mix_x, powers_x)
    f_h, f_l = halves(jnp.concatenate(entering, axis=0))
    high = mm(jnp.concatenate([f_h, f_l], axis=0), ty_v[r // 2, 0:256, :], NT)
    through = high[0:128] + (high[128:256] + mm(f_h, ty_v[r // 2, 256:512, :], NT))
    for i in range(PEERS):
        row_out2[i] = through[8 * i : 8 * i + 8]

    for peer in rows_to:
        row_copy(peer, r, *row2).start()

    row_in2[r] = row_out2[r]

    for row_peer, col_peer in zip(rows_to, cols_to):
        row_copy(row_peer, r, *row1).wait_send()
        corner_copy(row_peer, r).wait_send()
        col_copy(col_peer, c, *col1).wait_send()

    for l in range(EARLY, LEVELS):
        local_field(l)

    for row_peer, col_peer in zip(rows_to, cols_to):
        row_copy(row_peer, r, *row2).wait_send()
        col_copy(col_peer, c, *col2).wait_send()
    for peer in cols_to:
        col_copy(peer, peer, *col2).wait_recv()

    corners = [col_in2[i, 8:12, :] for i in range(PEERS)]
    state = weighted(corners, end_y)
    end = jnp.zeros(half, f32)
    for k in range(POLES):
        end += corner_mix_y[k][0:POLES] * jnp.broadcast_to(state[k : k + 1, :], half)
    turn = lambda t: pltpu.roll(jnp.concatenate([t, t], axis=0), 64, 1)
    enter = weighted(corners, enter_y) + back_y * turn(end)[0:POLES]
    twice = lambda t: jnp.concatenate([t, t], axis=0)
    enter_f = jnp.where(lane < 64, twice(enter), turn(enter))
    enter_b = jnp.where(lane < 64, turn(enter), twice(enter))
    corner_f = jnp.where(lane < 64, enter_f, slab_decay_y * enter_f + first)
    corner_b = jnp.where(lane < 64, slab_decay_y * enter_b + second, enter_b)
    corner = jnp.where(forward, corner_f, corner_b)

    spread_out = jnp.where(row_id // 8 == lane_id // 8, stack(corner), 0.0)
    k_h, k_l = halves(spread_out)
    ex_all = ex_v[...].reshape(64, BLOCK)
    x_h, x_l = halves(jnp.concatenate([ex_all, ex_all], axis=0))
    through = mm(k_h, x_h) + (mm(k_l, x_h) + mm(k_h, x_l))

    rounded = lambda t: t.astype(bf16).astype(f32)
    for l in range(LEVELS):
        decay = jnp.concatenate([decay_y[l], decay_y[l]], axis=1)
        enter = jnp.concatenate([col_in2[2 * l, 0:8, :], col_in2[2 * l + 1, 0:8, :]], axis=1)
        slabs = (
            jnp.where(forward_wide, enter, decay * enter + v_v[LEVELS + l]),
            jnp.where(forward_wide, decay * enter + v_v[l], enter),
        )
        e_h, e_l = halves(jnp.concatenate(slabs, axis=0))
        wide = mm(jnp.concatenate([e_h, e_l], axis=0), txh_v[l])
        wide = wide[0:16] + wide[16:32] + mm(e_h, txl_v[l])
        x_h = rounded(ex_v[l])
        x_l = ex_v[l] - x_h
        for s in range(2):
            at = 8 * (s * LEVELS + l)
            g = wide[8 * s : 8 * s + 8] + through[at : at + 8]
            g_h = rounded(g)
            g_l = g - g_h
            right_out[2 * l + s] = jnp.concatenate([x_h, x_h, x_l, g_h, g_l, g_h], axis=0).astype(bf16)

    for peer in rows_to:
        row_copy(peer, peer, *row2).wait_recv()

    for l in range(LEVELS):
        y_h = rounded(ey_v[l])
        y_l = ey_v[l] - y_h
        for s in range(2):
            f = row_in2[2 * l + s]
            f_h = rounded(f)
            f_l = f - f_h
            left_out[2 * l + s] = jnp.concatenate([f_h, f_l, f_h, y_h, y_h, y_l], axis=0).astype(bf16)


def kernel_field(p_ref, left_ref, right_ref, out_hbm, out_v, save_sem):
    save = lambda l: pltpu.make_async_copy(out_v.at[l], out_hbm.at[l], save_sem.at[l])

    for l in range(LEVELS):
        for s in range(2):
            rows = slice(BLOCK * s, BLOCK * (s + 1))
            out_v[l, rows, :] = jnp.exp(p_ref[l, rows, :] + mm(left_ref[2 * l + s], right_ref[2 * l + s], TN))
        save(l).start()

    @pl.loop(0, LEVELS)
    def _(l):
        save(l).wait()


def on_device(source, pole_x, weight_x, pole_y, weight_y):
    vmem = pl.BlockSpec(memory_space=pltpu.VMEM)
    hbm = pl.BlockSpec(memory_space=pltpu.HBM)
    shape = source.shape
    V = pltpu.VMEM
    sems = pltpu.SemaphoreType.DMA((PEERS,))
    local, left, right = pl.pallas_call(
        kernel_states,
        out_shape=(
            jax.ShapeDtypeStruct(shape, f32),
            jax.ShapeDtypeStruct((16, 48, BLOCK), bf16),
            jax.ShapeDtypeStruct((16, 48, BLOCK), bf16),
        ),
        in_specs=[hbm] * 5,
        out_specs=(vmem, vmem, vmem),
        scratch_shapes=[pltpu.SMEM((POLES, LEVELS), f32)] * 4 + [
            V(shape, f32), V(shape, bf16), V(shape, bf16), V(shape, bf16), V(shape, bf16),
            V((LEVELS, 512, BLOCK), bf16), V((LEVELS, 16, BLOCK), bf16), V((LEVELS, BLOCK, BLOCK), bf16), V((LEVELS, BLOCK, BLOCK), bf16),
            V((LEVELS, 16, BLOCK), bf16), V((64, BLOCK), f32), V((64, BLOCK), f32),
            V((LEVELS, 8, BLOCK), f32), V((LEVELS, 8, BLOCK), f32), V((LEVELS, 8, 128), f32),
            V((16, 8, BLOCK), f32),
            V((PEERS, 8, BLOCK), f32), V((PEERS, 8, BLOCK), f32), V((1, 8, 128), f32), V((PEERS, 8, 128), f32), V((PEERS, 8, 128), f32), V((PEERS, 8, 128), f32),
            V((PEERS, 8, BLOCK), f32), V((PEERS, 8, BLOCK), f32), V((PEERS, 16, 128), f32), V((PEERS, 16, 128), f32),
            pltpu.SemaphoreType.DMA((4,)), pltpu.SemaphoreType.DMA((LEVELS,)),
        ] + [sems] * 10,
        compiler_params=pltpu.CompilerParams(collective_id=0, has_side_effects=True, vmem_limit_bytes=48 * 2**20),
    )(*(pltpu.with_memory_space_constraint(t.T, pltpu.HBM) for t in (pole_x, weight_x, pole_y, weight_y)), source)
    return pl.pallas_call(
        kernel_field,
        out_shape=jax.ShapeDtypeStruct(shape, f32),
        in_specs=[vmem] * 3,
        out_specs=hbm,
        scratch_shapes=[V(shape, f32), pltpu.SemaphoreType.DMA((LEVELS,))],
        compiler_params=pltpu.CompilerParams(vmem_limit_bytes=24 * 2**20),
    )(local, left, right)


def solution(mesh):
    return jax.shard_map(
        on_device,
        mesh=mesh,
        in_specs=(P(None, "col", "row"), P(), P(), P(), P()),
        out_specs=P(None, "col", "row"),
        check_vma=False,
    )
```
